256 devices in a mesh: roll: 64 (over z, y, core), head: 4 (over x).
Axes of the slice: x: 4, y: 4, z: 8, core: 2. Of those that a mesh axis runs over, the one named last changes fastest.
Arguments:
- query: bfloat16 [64, 384, 3584], P('roll', None, 'head'), may hold values from -6 to 6
- key_suffix: bfloat16 [64, 384, 512], P('roll', None, 'head'), may hold values from -6 to 6
- value_suffix: bfloat16 [64, 384, 512], P('roll', None, 'head'), may hold values from -6 to 6
- key_prompt: bfloat16 [2, 2048, 512], P(None, 'roll', 'head'), may hold values from -6 to 6
- value_prompt: bfloat16 [2, 2048, 512], P(None, 'roll', 'head'), may hold values from -6 to 6
- attn_out: bfloat16 [64, 384, 3584], P('roll', None, 'head'), may hold values from -6 to 6
- grad_out: bfloat16 [64, 384, 3584], P('roll', 'head'), may hold values from -24 to 24
- log_norm: float32 [64, 28, 384], P('roll', 'head'), as said below
- prompt_id: int32 [64], P('roll'), may hold values from 0 to 1
- lengths: int32 [64], P('roll'), may hold values from 48 to 384, as said below
Outputs:
- grad_query: bfloat16 [64, 384, 3584], P('roll', None, 'head')
- grad_key_suffix: bfloat16 [64, 384, 512], P('roll', None, 'head')
- grad_value_suffix: bfloat16 [64, 384, 512], P('roll', None, 'head')
- grad_key_prompt: bfloat16 [2, 2048, 512], P(None, 'roll', 'head')
- grad_value_prompt: bfloat16 [2, 2048, 512], P(None, 'roll', 'head')
The draws below stay inside these ranges and needn't reach their ends.
Inputs may be any that keep to these rules, and one draw needn't show every extreme that they name: Valid lengths of the rollouts; some rollout has 384 valid tokens and some has 48. `log_norm`: one value a query row and head.
All inputs are finite; a program needn't handle non-finite values.
Results may differ from the reference program's by a relative error of at most 0.005.
Values may be sent and summed in bfloat16 or wider, within the bound.
No kernel may reach another device: no remote copies, remote signals or barrier semaphores. Data moves between devices by JAX's collectives and lax.ppermute only.
A program may use at most 64 MiB of HBM per device.

```python
import jax
import jax.numpy as jnp
from jax import lax

QH = 28
KVH = 4
DH = 128
SL = 384
PL = 2048
PROMPTS = 2
ROLLOUTS = 64


def draw_log_norm(key, part):
    key = jax.random.fold_in(key, 11)
    base_level = jnp.log(jnp.float32(PL + SL // 2)) + 0.5
    rising = jnp.log(1.0 + 2.0 * jnp.arange(ROLLOUTS, dtype=jnp.float32) / max(ROLLOUTS - 1, 1))
    jitter = jnp.clip(0.3 * jax.random.normal(key, (ROLLOUTS, QH, SL), jnp.float32), -1.0, 0.6)
    return base_level - rising[:, None, None] + jitter


def draw_lengths(key, part):
    key = jax.random.fold_in(key, 23)
    first_key, second_key, third_key = jax.random.split(key, 3)
    drawn = jax.random.randint(first_key, (ROLLOUTS,), SL // 8, SL + 1)
    full_slot = jax.random.randint(second_key, (), 0, ROLLOUTS)
    short_slot = (full_slot + 1 + jax.random.randint(third_key, (), 0, ROLLOUTS - 1)) % ROLLOUTS
    drawn = drawn.at[full_slot].set(SL)
    return drawn.at[short_slot].set(SL // 8)


def place_ends(entries, rng, least, high):
    shape = entries.shape
    spot = [jax.random.randint(jax.random.fold_in(rng, axis), (), 0, shape[axis]) for axis in range(len(shape))]
    entries = entries.at[tuple(spot)].set(least)
    longest = shape.index(max(shape))
    spot[longest] = (spot[longest] + 1) % shape[longest]
    return entries.at[tuple(spot)].set(high)


def shard_levels(key, dims, cuts, smallest, high):
    loudness, own = 1.0, jax.random.fold_in(key, 6)
    for axis_at, blocks in cuts:
        heights = jnp.exp(jax.random.uniform(jax.random.fold_in(own, axis_at), (blocks,), jnp.float32, smallest / len(cuts), high / len(cuts)))
        loudness = loudness * jnp.repeat(heights, dims[axis_at] // blocks).reshape([-1 if axis == axis_at else 1 for axis in range(len(dims))])
    return loudness


def noise(own_key, extent, deviation, bound, shards=(), kind=jnp.bfloat16):
    entries = jax.random.normal(own_key, extent, jnp.float32) * deviation
    if len(shards) > 0:
        entries = shard_levels(own_key, extent, shards, -0.22, 0.18) * entries
    return jnp.clip(entries, min=-bound, max=bound).astype(kind)


def setup_inputs(seed: int = 0) -> dict:
    streams_of = jax.random.split(jax.random.key(seed), 11)
    return {
        "query": noise(streams_of[0], (ROLLOUTS, SL, QH * DH), 1.0, 6.0, ((0, 64), (2, 4))),
        "key_suffix": noise(streams_of[1], (ROLLOUTS, SL, KVH * DH), 1.0, 6.0, ((0, 64), (2, 4))),
        "value_suffix": noise(streams_of[2], (ROLLOUTS, SL, KVH * DH), 1.0, 6.0, ((0, 64), (2, 4))),
        "key_prompt": noise(streams_of[3], (PROMPTS, PL, KVH * DH), 1.0, 6.0, ((1, 64), (2, 4))),
        "value_prompt": noise(streams_of[4], (PROMPTS, PL, KVH * DH), 1.0, 6.0, ((1, 64), (2, 4))),
        "attn_out": noise(streams_of[5], (ROLLOUTS, SL, QH * DH), 1.0, 6.0, ((0, 64), (2, 4))),
        "grad_out": noise(streams_of[6], (ROLLOUTS, SL, QH * DH), 4.0, 24.0, ((0, 64), (1, 4))),
        "log_norm": draw_log_norm(jax.random.fold_in(streams_of[10], 71), 0),
        "prompt_id": place_ends(jax.random.randint(streams_of[8], (ROLLOUTS,), 0, PROMPTS), jax.random.fold_in(streams_of[8], 1), 0, PROMPTS - 1).astype(jnp.int32),
        "lengths": draw_lengths(jax.random.fold_in(streams_of[10], 71), 0),
    }


def attend_grads(rows_query, rows_grad, norm_rows, row_delta, key_rows, value_rows, visible):
    score_scale = key_rows.shape[-1] ** -0.5
    scores = lax.dot_general(rows_query, key_rows, (((1,), (1,)), ((), ())), preferred_element_type=jnp.float32) * score_scale
    weights = jnp.exp(scores - norm_rows[:, None])
    if visible is not None:
        weights = jnp.where(visible, weights, jnp.zeros_like(weights))
    weight_grad = lax.dot_general(rows_grad, value_rows, (((1,), (1,)), ((), ())), preferred_element_type=jnp.float32)
    score_grad = (weights * (weight_grad - row_delta[:, None]) * score_scale).astype(jnp.bfloat16)
    weights_rounded = weights.astype(jnp.bfloat16)
    query_grad = jnp.dot(score_grad, key_rows, preferred_element_type=jnp.float32)
    key_grad = lax.dot_general(score_grad, rows_query, (((0,), (0,)), ((), ())), preferred_element_type=jnp.float32)
    value_grad = lax.dot_general(weights_rounded, rows_grad, (((0,), (0,)), ((), ())), preferred_element_type=jnp.float32)
    return query_grad, key_grad, value_grad


def rollout_grads(query, key_suffix, value_suffix, key_chosen, value_chosen, attn_out, grad_out, log_norm, length):
    group_size = QH // KVH
    row_count = SL * group_size
    position = jnp.arange(row_count) // group_size
    live_row = position < length
    causal = jnp.arange(SL)[None, :] <= position[:, None]
    visible = jnp.concatenate([jnp.ones((row_count, PL), bool), causal], 1)
    query_parts, key_parts, value_parts, prompt_keys, prompt_values = [], [], [], [], []
    for head_index in range(KVH):
        query_cols = slice(head_index * group_size * DH, (head_index + 1) * group_size * DH)
        key_cols = slice(head_index * DH, (head_index + 1) * DH)
        rows_query = query[:, query_cols].reshape(row_count, DH)
        rows_out = attn_out[:, query_cols].reshape(row_count, DH)
        rows_grad = grad_out[:, query_cols].reshape(row_count, DH)
        rows_grad = jnp.where(live_row[:, None], rows_grad, jnp.zeros_like(rows_grad))
        norm_rows = log_norm[head_index * group_size:(head_index + 1) * group_size].T.reshape(row_count)
        row_delta = jnp.sum(rows_grad.astype(jnp.float32) * rows_out.astype(jnp.float32), axis=1)
        key_rows = jnp.concatenate([key_chosen[:, key_cols], key_suffix[:, key_cols]], 0)
        value_rows = jnp.concatenate([value_chosen[:, key_cols], value_suffix[:, key_cols]], 0)
        query_grad, key_grad, value_grad = attend_grads(rows_query, rows_grad, norm_rows, row_delta, key_rows, value_rows, visible)
        query_parts.append(query_grad.reshape(SL, group_size * DH))
        key_parts.append(key_grad[PL:])
        value_parts.append(value_grad[PL:])
        prompt_keys.append(key_grad[:PL])
        prompt_values.append(value_grad[:PL])
    return (jnp.concatenate(query_parts, 1), jnp.concatenate(key_parts, 1), jnp.concatenate(value_parts, 1),
            jnp.concatenate(prompt_keys, 1), jnp.concatenate(prompt_values, 1))


def reference(query, key_suffix, value_suffix, key_prompt, value_prompt, attn_out, grad_out, log_norm, prompt_id, lengths):
    def per_rollout(prompt_acc, rollout_items):
        q_rows, k_rows, v_rows, out_rows, grad_rows, norm_rows, chosen, length = rollout_items
        key_chosen = lax.dynamic_index_in_dim(key_prompt, chosen, 0, keepdims=False)
        value_chosen = lax.dynamic_index_in_dim(value_prompt, chosen, 0, keepdims=False)
        query_grad, key_grad, value_grad, prompt_key, prompt_value = rollout_grads(
            q_rows, k_rows, v_rows, key_chosen, value_chosen, out_rows, grad_rows, norm_rows, length)
        prompt_mask = (jnp.arange(PROMPTS) == chosen).astype(jnp.float32)[:, None, None]
        new_acc = (prompt_acc[0] + prompt_mask * prompt_key[None], prompt_acc[1] + prompt_mask * prompt_value[None])
        return new_acc, (query_grad.astype(jnp.bfloat16), key_grad.astype(jnp.bfloat16), value_grad.astype(jnp.bfloat16))

    zeros_acc = jnp.zeros((PROMPTS, PL, KVH * DH), jnp.float32)
    (key_total, value_total), (grad_query, grad_key_suffix, grad_value_suffix) = lax.scan(
        per_rollout, (zeros_acc, zeros_acc),
        (query, key_suffix, value_suffix, attn_out, grad_out, log_norm, prompt_id, lengths))
    return (grad_query, grad_key_suffix, grad_value_suffix,
            key_total.astype(jnp.bfloat16), value_total.astype(jnp.bfloat16))
```

```python
import functools

import jax
import jax.numpy as jnp
from jax import lax
from jax.experimental import pallas as pl
from jax.experimental.pallas import tpu as pltpu
from jax.sharding import Mesh
from jax.sharding import PartitionSpec as P

BF16 = jnp.bfloat16
F32 = jnp.float32
GROUP = ("y", "c")


def score_blocks(key_rows, value_rows, query_t, grad_t, norm_row, delta_row, scale, visible=None):
    scores_t = jnp.dot(key_rows, query_t, preferred_element_type=F32) * scale
    weights_t = jnp.exp(scores_t - norm_row)
    if visible is not None:
        weights_t = jnp.where(visible, weights_t, jnp.zeros_like(weights_t))
    weight_grad_t = jnp.dot(value_rows, grad_t, preferred_element_type=F32)
    score_grad_t = (weights_t * (weight_grad_t - delta_row) * scale).astype(BF16)
    return weights_t.astype(BF16), score_grad_t


def suffix_kernel(
    length_ref, query_ref, out_ref, grad_ref, norm_ref, key_ref, value_ref,
    query_rows_ref, grad_rows_ref, query_t_ref, grad_t_ref, norm_row_ref, delta_row_ref,
    query_acc_ref, key_grad_ref, value_grad_ref,
):
    seq_len, width = key_ref.shape
    group_size = query_ref.shape[1] // width
    scale = width ** (-0.5)
    live_down = lax.broadcasted_iota(jnp.int32, (seq_len, width), 0) < length_ref[0]
    key_at = lax.broadcasted_iota(jnp.int32, (seq_len, seq_len), 0)
    query_at = lax.broadcasted_iota(jnp.int32, (seq_len, seq_len), 1)
    causal = key_at <= query_at
    key_rows, value_rows = key_ref[...], value_ref[...]
    key_t = key_rows.T
    key_acc = jnp.zeros((seq_len, width), F32)
    value_acc = jnp.zeros((seq_len, width), F32)
    for head in range(group_size):
        cols = slice(head * width, (head + 1) * width)
        rows = slice(head * seq_len, (head + 1) * seq_len)
        query_rows = query_ref[:, cols]
        grad_rows = grad_ref[:, cols]
        grad_rows = jnp.where(live_down, grad_rows, jnp.zeros_like(grad_rows))
        query_t, grad_t = query_rows.T, grad_rows.T
        out_t = out_ref[:, cols].T
        delta_row = jnp.sum(grad_t.astype(F32) * out_t.astype(F32), axis=0, keepdims=True)
        norm_row = norm_ref[head : head + 1, :]
        query_rows_ref[rows, :] = query_rows
        grad_rows_ref[rows, :] = grad_rows
        query_t_ref[:, rows] = query_t
        grad_t_ref[:, rows] = grad_t
        norm_row_ref[:, rows] = norm_row
        delta_row_ref[:, rows] = delta_row
        weights_t, score_grad_t = score_blocks(
            key_rows, value_rows, query_t, grad_t, norm_row, delta_row, scale, causal
        )
        query_acc_ref[:, rows] = jnp.dot(key_t, score_grad_t, preferred_element_type=F32)
        key_acc += jnp.dot(score_grad_t, query_rows, preferred_element_type=F32)
        value_acc += jnp.dot(weights_t, grad_rows, preferred_element_type=F32)
    key_grad_ref[...] = key_acc.astype(BF16)
    value_grad_ref[...] = value_acc.astype(BF16)


def suffix_part(length, query, attn_out, grad, log_norm, key_suffix, value_suffix):
    seq_len, width = key_suffix.shape
    row_count = query.shape[0] * query.shape[1] // width
    shape = jax.ShapeDtypeStruct
    vmem = pl.BlockSpec(memory_space=pltpu.VMEM)
    return pl.pallas_call(
        suffix_kernel,
        in_specs=[pl.BlockSpec(memory_space=pltpu.SMEM)] + [vmem] * 6,
        out_specs=[vmem] * 9,
        out_shape=[
            shape((row_count, width), BF16),
            shape((row_count, width), BF16),
            shape((width, row_count), BF16),
            shape((width, row_count), BF16),
            shape((1, row_count), F32),
            shape((1, row_count), F32),
            shape((width, row_count), F32),
            shape((seq_len, width), BF16),
            shape((seq_len, width), BF16),
        ],
        compiler_params=pltpu.CompilerParams(vmem_limit_bytes=48 * 1024 * 1024),
        name="suffix_part",
    )(length, query, attn_out, grad, log_norm, key_suffix, value_suffix)


def prompt_kernel(
    query_rows_ref, grad_rows_ref, query_t_ref, grad_t_ref, norm_row_ref, delta_row_ref,
    query_acc_ref, pair_ref, query_grad_ref, pair_grad_ref, acc_ref, *, blocks,
):
    width = query_rows_ref.shape[1]
    scale = width ** (-0.5)
    step = pl.program_id(0)

    @pl.when(step == 0)
    def _():
        acc_ref[...] = query_acc_ref[...]

    key_rows, value_rows = pair_ref[0, 0], pair_ref[0, 1]
    key_t = key_rows.T
    key_acc = jnp.zeros(key_rows.shape, F32)
    value_acc = jnp.zeros(key_rows.shape, F32)
    for rows in blocks:
        weights_t, score_grad_t = score_blocks(
            key_rows, value_rows, query_t_ref[:, rows], grad_t_ref[:, rows],
            norm_row_ref[:, rows], delta_row_ref[:, rows], scale,
        )
        acc_ref[:, rows] += jnp.dot(key_t, score_grad_t, preferred_element_type=F32)
        key_acc += jnp.dot(score_grad_t, query_rows_ref[rows, :], preferred_element_type=F32)
        value_acc += jnp.dot(weights_t, grad_rows_ref[rows, :], preferred_element_type=F32)
    pair_grad_ref[0, 0] = key_acc.astype(BF16)
    pair_grad_ref[0, 1] = value_acc.astype(BF16)

    @pl.when(step == pl.num_programs(0) - 1)
    def _():
        seq_len = query_grad_ref.shape[0]
        for head in range(query_grad_ref.shape[1] // width):
            part = acc_ref[:, head * seq_len : (head + 1) * seq_len]
            query_grad_ref[:, head * width : (head + 1) * width] = part.T.astype(BF16)


def prompt_part(rows, query_acc, pair, seq_len):
    row_count, width = rows[0].shape
    wide = 2 * seq_len
    blocks = [slice(at, min(at + wide, row_count)) for at in range(0, row_count, wide)]
    whole = pl.BlockSpec(memory_space=pltpu.VMEM)
    tile = pl.BlockSpec((1,) + pair.shape[1:], lambda i: (i, 0, 0, 0))
    out_shape = (seq_len, row_count * width // seq_len)
    return pl.pallas_call(
        functools.partial(prompt_kernel, blocks=blocks),
        grid=(pair.shape[0],),
        in_specs=[whole] * 7 + [tile],
        out_specs=[pl.BlockSpec(out_shape, lambda i: (0, 0)), tile],
        out_shape=[jax.ShapeDtypeStruct(out_shape, BF16), jax.ShapeDtypeStruct(pair.shape, BF16)],
        scratch_shapes=[pltpu.VMEM((width, row_count), F32)],
        compiler_params=pltpu.CompilerParams(vmem_limit_bytes=48 * 1024 * 1024),
        name="prompt_part",
    )(*rows, query_acc, pair)


def exchange(blocks, axes):
    return lax.all_to_all(blocks, axes, split_axis=0, concat_axis=0, tiled=True)


def per_device(
    query, key_suffix, value_suffix, key_prompt, value_prompt, attn_out, grad_out, log_norm,
    prompt_id, lengths,
):
    seq_len, columns = query.shape[1:]
    width = key_suffix.shape[2]
    prompt_count, owned = key_prompt.shape[:2]
    heads, stacks, group = lax.axis_size("head"), lax.axis_size("z"), lax.axis_size(GROUP)

    grad_parts = [grad_out[0][:, columns * i : columns * (i + 1)] for i in range(heads)]
    grad_local = exchange(jnp.concatenate(grad_parts, 0), "head")

    own_pair = jnp.stack([key_prompt, value_prompt], 1).reshape(1, -1, width)
    stacked = exchange(jnp.broadcast_to(own_pair, (stacks,) + own_pair.shape[1:]), "z")
    ids = exchange(jnp.broadcast_to(prompt_id[:, None], (group, 128)), GROUP)[:, 0]
    stacked = stacked.reshape(stacks, prompt_count, 2, owned, width)
    stacked = stacked.transpose(1, 2, 0, 3, 4).reshape(prompt_count, 2, stacks * owned, width)
    wanted = (ids == 0)[:, None, None, None]
    pair = exchange(jnp.where(wanted, stacked[:1], stacked[1:]), GROUP)

    *rows, query_acc, key_grad, value_grad = suffix_part(
        lengths, query[0], attn_out[0], grad_local, log_norm[0], key_suffix[0], value_suffix[0]
    )
    query_grad, pair_grad = prompt_part(rows, query_acc, pair, seq_len)

    shares = exchange(pair_grad, GROUP).astype(F32)
    totals = jnp.stack(
        [
            jnp.sum(jnp.where((ids == i)[:, None, None, None], shares, 0.0), 0)
            for i in range(prompt_count)
        ],
        0,
    )
    totals = totals.reshape(prompt_count, 2, stacks, owned, width).transpose(2, 0, 1, 3, 4)
    totals = totals.astype(BF16).reshape(stacks, -1, width)
    final = jnp.sum(exchange(totals, "z").astype(F32), 0).astype(BF16)
    final = final.reshape(prompt_count, 2, owned, width)
    return (query_grad[None], key_grad[None], value_grad[None], final[:, 0], final[:, 1])


def solution(mesh):
    roll, head = mesh.devices.shape
    fine = Mesh(mesh.devices.reshape(roll // 8, 4, 2, head), ("z", "y", "c", "head"))
    rolls = ("z", "y", "c")
    by_rollout = P(rolls, None, "head")
    by_key = P(None, rolls, "head")
    by_row = P(rolls, "head", None)
    in_specs = (
        by_rollout, by_rollout, by_rollout, by_key, by_key, by_rollout, by_row, by_row,
        P(rolls), P(rolls),
    )
    out_specs = (by_rollout, by_rollout, by_rollout, by_key, by_key)
    return jax.shard_map(
        per_device, mesh=fine, in_specs=in_specs, out_specs=out_specs, check_vma=False
    )
```

```python
import functools

import jax
import jax.numpy as jnp
from jax import lax
from jax.experimental import pallas as pl
from jax.experimental.pallas import tpu as pltpu
from jax.sharding import Mesh
from jax.sharding import PartitionSpec as P

BF16 = jnp.bfloat16
F32 = jnp.float32
GROUP = ("y", "c")
LOG2E = 1.4426950408889634
VMEM = pl.BlockSpec(memory_space=pltpu.VMEM)
SMEM = pl.BlockSpec(memory_space=pltpu.SMEM)
PARAMS = pltpu.CompilerParams(vmem_limit_bytes=28 * 1024 * 1024)
MARK = 16


def cost(row_count, key_count, width):
    pairs = row_count * key_count
    return pl.CostEstimate(
        flops=10 * pairs * width, bytes_accessed=16 * row_count * width, transcendentals=pairs
    )


def score_blocks(key_rows, value_rows, query_t, grad_t, norm_row, delta_row, visible=None):
    scale = key_rows.shape[1] ** (-0.5)
    scores_t = jnp.dot(key_rows, query_t, preferred_element_type=F32)
    weights_t = jnp.exp2(scores_t * (scale * LOG2E) - norm_row)
    if visible is not None:
        weights_t = jnp.where(visible, weights_t, jnp.zeros_like(weights_t))
    weight_grad_t = jnp.dot(value_rows, grad_t, preferred_element_type=F32)
    score_grad_t = (weights_t * (weight_grad_t - delta_row) * scale).astype(BF16)
    return weights_t.astype(BF16), score_grad_t


def suffix_kernel(
    length_ref, place_ref, query_ref, out_ref, norm_ref, key_ref, value_ref, *refs
):
    grad_refs, refs = refs[:-10], refs[-10:]
    (
        query_rows_ref, grad_rows_ref, query_t_ref, grad_t_ref, norm_row_ref, delta_row_ref,
        query_acc_ref, key_grad_ref, value_grad_ref, grad_ref,
    ) = refs
    seq_len, width = key_ref.shape
    group_size = query_ref.shape[1] // width
    part = grad_refs[0].shape[0]
    for i, piece in enumerate(grad_refs):
        start = pl.multiple_of((place_ref[0] ^ i) * part, part)
        grad_ref[pl.ds(start, part), :] = piece[...]
    live_down = lax.broadcasted_iota(jnp.int32, (seq_len, width), 0) < length_ref[0]
    key_at = lax.broadcasted_iota(jnp.int32, (seq_len, seq_len), 0)
    query_at = lax.broadcasted_iota(jnp.int32, (seq_len, seq_len), 1)
    causal = key_at <= query_at
    key_rows, value_rows = key_ref[...], value_ref[...]
    key_t = key_rows.T
    key_acc = jnp.zeros((seq_len, width), F32)
    value_acc = jnp.zeros((seq_len, width), F32)
    for head in range(group_size):
        cols = slice(head * width, (head + 1) * width)
        rows = slice(head * seq_len, (head + 1) * seq_len)
        query_rows = query_ref[:, cols]
        grad_rows = grad_ref[:, cols]
        grad_rows = jnp.where(live_down, grad_rows, jnp.zeros_like(grad_rows))
        query_t, grad_t = query_rows.T, grad_rows.T
        out_t = out_ref[:, cols].T
        delta_row = jnp.sum(grad_t.astype(F32) * out_t.astype(F32), axis=0, keepdims=True)
        norm_row = norm_ref[head : head + 1, :] * LOG2E
        query_rows_ref[rows, :] = query_rows
        grad_rows_ref[rows, :] = grad_rows
        query_t_ref[:, rows] = query_t
        grad_t_ref[:, rows] = grad_t
        norm_row_ref[:, rows] = norm_row
        delta_row_ref[:, rows] = delta_row
        weights_t, score_grad_t = score_blocks(
            key_rows, value_rows, query_t, grad_t, norm_row, delta_row, causal
        )
        query_acc_ref[:, rows] = jnp.dot(key_t, score_grad_t, preferred_element_type=F32)
        key_acc += jnp.dot(score_grad_t, query_rows, preferred_element_type=F32)
        value_acc += jnp.dot(weights_t, grad_rows, preferred_element_type=F32)
    key_grad_ref[...] = key_acc.astype(BF16)
    value_grad_ref[...] = value_acc.astype(BF16)


def suffix_part(length, place, query, attn_out, log_norm, key_suffix, value_suffix, grads):
    seq_len, width = key_suffix.shape
    row_count = query.shape[0] * query.shape[1] // width
    shape = jax.ShapeDtypeStruct
    return pl.pallas_call(
        suffix_kernel,
        in_specs=[SMEM, SMEM] + [VMEM] * (5 + len(grads)),
        out_specs=[VMEM] * 9,
        out_shape=[
            shape((row_count, width), BF16),
            shape((row_count, width), BF16),
            shape((width, row_count), BF16),
            shape((width, row_count), BF16),
            shape((1, row_count), F32),
            shape((1, row_count), F32),
            shape((width, row_count), F32),
            shape((seq_len, width), BF16),
            shape((seq_len, width), BF16),
        ],
        scratch_shapes=[pltpu.VMEM(query.shape, BF16)],
        compiler_params=PARAMS,
        cost_estimate=cost(row_count, seq_len, width),
        name="suffix_part",
    )(length, place, query, attn_out, log_norm, key_suffix, value_suffix, *grads)


def prompt_kernel(
    chosen_ref, core_ref, query_rows_ref, grad_rows_ref, query_t_ref, grad_t_ref, norm_row_ref,
    delta_row_ref, query_acc_ref, pair_ref, *refs, blocks, last,
):
    query_grad_ref, pair_grad_ref = refs[-2:]
    places, _, _, count, width = pair_ref.shape
    chosen = chosen_ref[0]
    key_rows = pair_ref[:, chosen, 0].reshape(places * count, width)
    value_rows = pair_ref[:, chosen, 1].reshape(places * count, width)
    key_t = key_rows.T
    key_acc = jnp.zeros(key_rows.shape, F32)
    value_acc = jnp.zeros(key_rows.shape, F32)
    for head, rows in enumerate(blocks):
        weights_t, score_grad_t = score_blocks(
            key_rows, value_rows, query_t_ref[:, rows], grad_t_ref[:, rows],
            norm_row_ref[:, rows], delta_row_ref[:, rows],
        )
        query_part = jnp.dot(key_t, score_grad_t, preferred_element_type=F32)
        query_part += query_acc_ref[:, rows]
        if last:
            query_grad_ref[:, head * width : (head + 1) * width] = query_part.T.astype(BF16)
        else:
            query_grad_ref[:, rows] = query_part
        key_acc += jnp.dot(score_grad_t, query_rows_ref[rows, :], preferred_element_type=F32)
        value_acc += jnp.dot(weights_t, grad_rows_ref[rows, :], preferred_element_type=F32)
    key_grad = key_acc.astype(BF16).reshape(places, count, width)
    value_grad = value_acc.astype(BF16).reshape(places, count, width)
    if not last:
        pair_grad_ref[:, :count] = key_grad
        pair_grad_ref[:, count:] = value_grad
        return
    core = core_ref[0]
    mark = jnp.full((MARK, width), chosen.astype(F32), F32).astype(BF16)
    for i in range(places):
        mine, other = 2 * i + core, 2 * i + 1 - core
        pair_grad_ref[mine, : 2 * count] = refs[0][i]
        pair_grad_ref[other, :count] = key_grad[i]
        pair_grad_ref[other, count : 2 * count] = value_grad[i]
        pair_grad_ref[mine, 2 * count :] = mark
        pair_grad_ref[other, 2 * count :] = mark


def prompt_part(chosen, core, rows, query_acc, pair, seq_len, earlier=None):
    last = earlier is not None
    row_count, width = rows[0].shape
    blocks = [slice(at, at + seq_len) for at in range(0, row_count, seq_len)]
    out = jax.ShapeDtypeStruct((width, row_count), F32)
    places, _, _, count, _ = pair.shape
    pair_out = jax.ShapeDtypeStruct((places, 2 * count, width), BF16)
    more = []
    if last:
        out = jax.ShapeDtypeStruct((seq_len, row_count * width // seq_len), BF16)
        pair_out = jax.ShapeDtypeStruct((2 * places, 2 * count + MARK, width), BF16)
        more = [earlier]
    return pl.pallas_call(
        functools.partial(prompt_kernel, blocks=blocks, last=last),
        in_specs=[SMEM, SMEM] + [VMEM] * (8 + len(more)),
        out_specs=[VMEM] * 2,
        out_shape=[out, pair_out],
        compiler_params=PARAMS,
        cost_estimate=cost(row_count, places * count, width),
        name="prompt_last" if last else "prompt_first",
    )(chosen, core, *rows, query_acc, pair, *more)


def exchange(blocks, axes):
    return lax.all_to_all(blocks, axes, split_axis=0, concat_axis=0, tiled=True)


def swap(block, axis, flip):
    return lax.ppermute(block, axis, [(i, i ^ flip) for i in range(lax.axis_size(axis))])


def copies(block, count):
    return jnp.broadcast_to(block[None], (count,) + block.shape)


def per_device(
    query, key_suffix, value_suffix, key_prompt, value_prompt, attn_out, grad_out, log_norm,
    prompt_id, lengths,
):
    seq_len, columns = query.shape[1:]
    width = key_suffix.shape[2]
    prompt_count, owned = key_prompt.shape[:2]
    heads, stacks, lines = lax.axis_size("head"), lax.axis_size("z"), lax.axis_size("y")
    place, core = lax.axis_index("head"), lax.axis_index("c")[None]

    grads = []
    for i in range(heads):
        at = (place ^ i) * columns
        piece = lax.dynamic_slice_in_dim(grad_out[0], at, columns, axis=1)
        grads.append(swap(piece, "head", i) if i else piece)

    own_pair = jnp.stack([key_prompt, value_prompt], 1).reshape(-1, width)
    stacked = exchange(copies(own_pair, stacks).reshape(-1, width), "z")
    stacked, *grads = lax.optimization_barrier((stacked, *grads))
    stacked = stacked.reshape(stacks, prompt_count, 2, owned, width)
    stacked = stacked.transpose(1, 2, 0, 3, 4).reshape(-1, width)
    pair = exchange(copies(stacked, lines).reshape(-1, width), "y")
    pair = pair.reshape(lines, prompt_count, 2, stacks * owned, width)

    *rows, query_acc, key_grad, value_grad = suffix_part(
        lengths, place[None], query[0], attn_out[0], log_norm[0], key_suffix[0], value_suffix[0],
        grads,
    )
    pair, key_grad = lax.optimization_barrier((pair, key_grad))
    other_pair = swap(pair, "c", 1)
    query_acc, earlier = prompt_part(prompt_id, core, rows, query_acc, pair, seq_len)
    query_grad, pair_grad = prompt_part(
        prompt_id, core, rows, query_acc, other_pair, seq_len, earlier
    )

    shares = exchange(pair_grad, GROUP)
    ids = shares[:, -MARK : 1 - MARK, :1]
    shares = shares[:, :-MARK].astype(F32)
    totals = jnp.stack(
        [jnp.sum(jnp.where(ids == i, shares, 0.0), 0) for i in range(prompt_count)], 0
    )
    totals = totals.reshape(prompt_count, 2, stacks, owned, width).transpose(2, 0, 1, 3, 4)
    totals = totals.astype(BF16).reshape(stacks, -1, width)
    final = jnp.sum(exchange(totals, "z").astype(F32), 0).astype(BF16)
    final = final.reshape(prompt_count, 2, owned, width)
    return (query_grad[None], key_grad[None], value_grad[None], final[:, 0], final[:, 1])


def solution(mesh):
    roll, head = mesh.devices.shape
    fine = Mesh(mesh.devices.reshape(roll // 8, 4, 2, head), ("z", "y", "c", "head"))
    rolls = ("z", "y", "c")
    by_rollout = P(rolls, None, "head")
    by_key = P(None, rolls, "head")
    by_row = P(rolls, "head", None)
    in_specs = (
        by_rollout, by_rollout, by_rollout, by_key, by_key, by_rollout, by_row, by_row,
        P(rolls), P(rolls),
    )
    out_specs = (by_rollout, by_rollout, by_rollout, by_key, by_key)
    return jax.shard_map(
        per_device, mesh=fine, in_specs=in_specs, out_specs=out_specs, check_vma=False
    )
```

```python
import functools

import jax
import jax.numpy as jnp
from jax import lax
from jax.experimental import pallas as pl
from jax.experimental.pallas import tpu as pltpu
from jax.sharding import Mesh
from jax.sharding import PartitionSpec as P

BF16 = jnp.bfloat16
F32 = jnp.float32
GROUP = ("y", "c")
LOG2E = 1.4426950408889634
VMEM = pl.BlockSpec(memory_space=pltpu.VMEM)
SMEM = pl.BlockSpec(memory_space=pltpu.SMEM)
PARAMS = pltpu.CompilerParams(vmem_limit_bytes=28 * 1024 * 1024)
MARK = 16


def cost(row_count, key_count, width):
    pairs = row_count * key_count
    return pl.CostEstimate(
        flops=10 * pairs * width, bytes_accessed=16 * row_count * width, transcendentals=pairs
    )


def score_blocks(key_rows, value_rows, query_t, grad_t, norm_row, delta_row, visible=None):
    scale = key_rows.shape[1] ** (-0.5)
    scores_t = jnp.dot(key_rows, query_t, preferred_element_type=F32)
    weights_t = jnp.exp2(scores_t * (scale * LOG2E) - norm_row)
    if visible is not None:
        weights_t = jnp.where(visible, weights_t, jnp.zeros_like(weights_t))
    weight_grad_t = jnp.dot(value_rows, grad_t, preferred_element_type=F32)
    score_grad_t = (weights_t * (weight_grad_t - delta_row) * scale).astype(BF16)
    return weights_t.astype(BF16), score_grad_t


def suffix_kernel(
    info_ref, query_ref, out_ref, norm_ref, key_ref, value_ref, *refs
):
    grad_refs, refs = refs[:-10], refs[-10:]
    (
        query_rows_ref, grad_rows_ref, query_t_ref, grad_t_ref, norm_row_ref, delta_row_ref,
        query_acc_ref, key_grad_ref, value_grad_ref, grad_ref,
    ) = refs
    seq_len, width = key_ref.shape
    group_size = query_ref.shape[1] // width
    part = grad_refs[0].shape[0]
    for i, piece in enumerate(grad_refs):
        start = pl.multiple_of((info_ref[3] ^ i) * part, part)
        grad_ref[pl.ds(start, part), :] = piece[...]
    live_down = lax.broadcasted_iota(jnp.int32, (seq_len, width), 0) < info_ref[4]
    key_at = lax.broadcasted_iota(jnp.int32, (seq_len, seq_len), 0)
    query_at = lax.broadcasted_iota(jnp.int32, (seq_len, seq_len), 1)
    causal = key_at <= query_at
    key_rows, value_rows = key_ref[...], value_ref[...]
    key_t = key_rows.T
    key_acc = jnp.zeros((seq_len, width), F32)
    value_acc = jnp.zeros((seq_len, width), F32)
    for head in range(group_size):
        cols = slice(head * width, (head + 1) * width)
        rows = slice(head * seq_len, (head + 1) * seq_len)
        query_rows = query_ref[:, cols]
        grad_rows = grad_ref[:, cols]
        grad_rows = jnp.where(live_down, grad_rows, jnp.zeros_like(grad_rows))
        query_t, grad_t = query_rows.T, grad_rows.T
        out_t = out_ref[:, cols].T
        delta_row = jnp.sum(grad_t.astype(F32) * out_t.astype(F32), axis=0, keepdims=True)
        norm_row = norm_ref[head : head + 1, :] * LOG2E
        query_rows_ref[rows, :] = query_rows
        grad_rows_ref[rows, :] = grad_rows
        query_t_ref[:, rows] = query_t
        grad_t_ref[:, rows] = grad_t
        norm_row_ref[:, rows] = norm_row
        delta_row_ref[:, rows] = delta_row
        weights_t, score_grad_t = score_blocks(
            key_rows, value_rows, query_t, grad_t, norm_row, delta_row, causal
        )
        query_acc_ref[:, rows] = jnp.dot(key_t, score_grad_t, preferred_element_type=F32)
        key_acc += jnp.dot(score_grad_t, query_rows, preferred_element_type=F32)
        value_acc += jnp.dot(weights_t, grad_rows, preferred_element_type=F32)
    key_grad_ref[...] = key_acc.astype(BF16)
    value_grad_ref[...] = value_acc.astype(BF16)


def suffix_part(info, query, attn_out, log_norm, key_suffix, value_suffix, grads):
    seq_len, width = key_suffix.shape
    row_count = query.shape[0] * query.shape[1] // width
    shape = jax.ShapeDtypeStruct
    return pl.pallas_call(
        suffix_kernel,
        in_specs=[SMEM] + [VMEM] * (5 + len(grads)),
        out_specs=[VMEM] * 9,
        out_shape=[
            shape((row_count, width), BF16),
            shape((row_count, width), BF16),
            shape((width, row_count), BF16),
            shape((width, row_count), BF16),
            shape((1, row_count), F32),
            shape((1, row_count), F32),
            shape((width, row_count), F32),
            shape((seq_len, width), BF16),
            shape((seq_len, width), BF16),
        ],
        scratch_shapes=[pltpu.VMEM(query.shape, BF16)],
        compiler_params=PARAMS,
        cost_estimate=cost(row_count, seq_len, width),
        name="suffix_part",
    )(info, query, attn_out, log_norm, key_suffix, value_suffix, *grads)


def prompt_kernel(info_ref, *refs, blocks, count, earlier):
    pair_refs, refs = refs[:count], refs[count:]
    (
        query_rows_ref, grad_rows_ref, query_t_ref, grad_t_ref, norm_row_ref, delta_row_ref,
        query_acc_ref,
    ) = refs[:7]
    earlier_refs, (query_grad_ref, pair_grad_ref) = refs[7:-2], refs[-2:]
    chosen = info_ref[0]
    width = query_rows_ref.shape[1]

    def rows_of(which):
        parts = [ref[:, chosen, which] for ref in pair_refs]
        return jnp.concatenate([part.reshape(-1, width) for part in parts], 0)

    key_rows, value_rows = rows_of(0), rows_of(1)
    key_t = key_rows.T
    key_acc = jnp.zeros(key_rows.shape, F32)
    value_acc = jnp.zeros(key_rows.shape, F32)
    for head, rows in enumerate(blocks):
        weights_t, score_grad_t = score_blocks(
            key_rows, value_rows, query_t_ref[:, rows], grad_t_ref[:, rows],
            norm_row_ref[:, rows], delta_row_ref[:, rows],
        )
        query_part = jnp.dot(key_t, score_grad_t, preferred_element_type=F32)
        query_part += query_acc_ref[:, rows]
        if earlier:
            query_grad_ref[:, head * width : (head + 1) * width] = query_part.T.astype(BF16)
        else:
            query_grad_ref[:, rows] = query_part
        key_acc += jnp.dot(score_grad_t, query_rows_ref[rows, :], preferred_element_type=F32)
        value_acc += jnp.dot(weights_t, grad_rows_ref[rows, :], preferred_element_type=F32)
    size = key_rows.shape[0] // count
    key_grad, value_grad = key_acc.astype(BF16), value_acc.astype(BF16)
    own = [
        (key_grad[i * size : (i + 1) * size], value_grad[i * size : (i + 1) * size])
        for i in range(count)
    ]
    if not earlier:
        for i in range(count):
            pair_grad_ref[i, 0], pair_grad_ref[i, 1] = own[i]
        return
    core, line = info_ref[1], info_ref[2]
    lines = pair_grad_ref.shape[0] // 2
    mark = jnp.full((MARK, width), chosen.astype(F32), F32).astype(BF16)
    found = [(ref, i) for ref in earlier_refs for i in range(ref.shape[0])]
    found = [(ref[i, 0], ref[i, 1]) for ref, i in found] + own
    for (steps, other), (keys, values) in zip(earlier, found, strict=True):
        owner = 2 * lax.rem(line - steps + lines, lines) + (1 - core if other else core)
        pair_grad_ref[owner, :size] = keys
        pair_grad_ref[owner, size : 2 * size] = values
        pair_grad_ref[owner, 2 * size :] = mark


def prompt_part(info, pairs, rows, query_acc, seq_len, earlier=(), order=()):
    row_count, width = rows[0].shape
    blocks = [slice(at, at + seq_len) for at in range(0, row_count, seq_len)]
    stacks, _, _, owned, _ = pairs[0].shape
    size = stacks * owned
    out = jax.ShapeDtypeStruct((width, row_count), F32)
    pair_out = jax.ShapeDtypeStruct((len(pairs), 2, size, width), BF16)
    if order:
        out = jax.ShapeDtypeStruct((seq_len, row_count * width // seq_len), BF16)
        pair_out = jax.ShapeDtypeStruct((len(order), 2 * size + MARK, width), BF16)
    return pl.pallas_call(
        functools.partial(prompt_kernel, blocks=blocks, count=len(pairs), earlier=order),
        in_specs=[SMEM] + [VMEM] * (len(pairs) + 7 + len(earlier)),
        out_specs=[VMEM] * 2,
        out_shape=[out, pair_out],
        compiler_params=PARAMS,
        cost_estimate=cost(row_count, len(pairs) * size, width),
        name="prompt_part",
    )(info, *pairs, *rows, query_acc, *earlier)


def exchange(blocks, axes):
    return lax.all_to_all(blocks, axes, split_axis=0, concat_axis=0, tiled=True)


def trade(block, axis, target):
    return lax.ppermute(block, axis, [(i, target(i)) for i in range(lax.axis_size(axis))])


def copies(block, count):
    return jnp.broadcast_to(block[None], (count,) + block.shape)


def per_device(
    query, key_suffix, value_suffix, key_prompt, value_prompt, attn_out, grad_out, log_norm,
    prompt_id, lengths,
):
    seq_len, columns = query.shape[1:]
    width = key_suffix.shape[2]
    prompt_count, owned = key_prompt.shape[:2]
    heads, stacks, lines = lax.axis_size("head"), lax.axis_size("z"), lax.axis_size("y")
    place = lax.axis_index("head")
    info = jnp.stack(
        [prompt_id[0], lax.axis_index("c"), lax.axis_index("y"), place, lengths[0]]
    ).astype(jnp.int32)

    own_pair = jnp.stack([key_prompt, value_prompt], 1).reshape(-1, width)
    stacked = exchange(copies(own_pair, stacks).reshape(-1, width), "z")
    grads = []
    for i in range(heads):
        at = (place ^ i) * columns
        piece = lax.dynamic_slice_in_dim(grad_out[0], at, columns, axis=1)
        grads.append(trade(piece, "head", lambda j, i=i: j ^ i) if i else piece)
    stacked, info, *grads = lax.optimization_barrier((stacked, info, *grads))
    stacked = stacked.reshape(stacks, prompt_count, 2, owned, width)

    moved = {
        steps: trade(stacked, "y", lambda j, steps=steps: (j + steps) % lines)
        for steps in (1, lines - 1, 2)
    }
    *rows, query_acc, key_grad, value_grad = suffix_part(
        info, query[0], attn_out[0], log_norm[0], key_suffix[0], value_suffix[0], grads
    )
    near, key_grad = lax.optimization_barrier(([stacked, moved[1], moved[lines - 1]], key_grad))
    near_other = [trade(block, "c", lambda j: j ^ 1) for block in near]
    query_acc, first = prompt_part(info, near, rows, query_acc, seq_len)
    far, query_acc = lax.optimization_barrier((moved[2], query_acc))
    far_other = trade(far, "c", lambda j: j ^ 1)
    query_acc, second = prompt_part(info, near_other, rows, query_acc, seq_len)
    order = [(steps, other) for other in (False, True) for steps in (0, 1, lines - 1)]
    order += [(2, False), (2, True)]
    query_grad, pair_grad = prompt_part(
        info, [far, far_other], rows, query_acc, seq_len, (first, second), order
    )

    shares = exchange(pair_grad, GROUP)
    ids = shares[:, -MARK : 1 - MARK, :1]
    shares = shares[:, :-MARK].astype(F32)
    totals = jnp.stack(
        [jnp.sum(jnp.where(ids == i, shares, 0.0), 0) for i in range(prompt_count)], 0
    )
    totals = totals.reshape(prompt_count, 2, stacks, owned, width).transpose(2, 0, 1, 3, 4)
    totals = totals.astype(BF16).reshape(stacks, -1, width)
    final = jnp.sum(exchange(totals, "z").astype(F32), 0).astype(BF16)
    final = final.reshape(prompt_count, 2, owned, width)
    return (query_grad[None], key_grad[None], value_grad[None], final[:, 0], final[:, 1])


def solution(mesh):
    roll, head = mesh.devices.shape
    fine = Mesh(mesh.devices.reshape(roll // 8, 4, 2, head), ("z", "y", "c", "head"))
    rolls = ("z", "y", "c")
    by_rollout = P(rolls, None, "head")
    by_key = P(None, rolls, "head")
    by_row = P(rolls, "head", None)
    in_specs = (
        by_rollout, by_rollout, by_rollout, by_key, by_key, by_rollout, by_row, by_row,
        P(rolls), P(rolls),
    )
    out_specs = (by_rollout, by_rollout, by_rollout, by_key, by_key)
    return jax.shard_map(
        per_device, mesh=fine, in_specs=in_specs, out_specs=out_specs, check_vma=False
    )
```

```python
import functools

import jax
import jax.numpy as jnp
from jax import lax
from jax.experimental import pallas as pl
from jax.experimental.pallas import tpu as pltpu
from jax.sharding import Mesh
from jax.sharding import PartitionSpec as P

BF16 = jnp.bfloat16
F32 = jnp.float32
GROUP = ("y", "c")
LOG2E = 1.4426950408889634
VMEM = pl.BlockSpec(memory_space=pltpu.VMEM)
SMEM = pl.BlockSpec(memory_space=pltpu.SMEM)
PARAMS = pltpu.CompilerParams(vmem_limit_bytes=28 * 1024 * 1024)
MARK = 16


def cost(row_count, key_count, width):
    pairs = row_count * key_count
    return pl.CostEstimate(
        flops=10 * pairs * width, bytes_accessed=16 * row_count * width, transcendentals=pairs
    )


def score_blocks(key_rows, value_rows, query_t, grad_t, norm_row, delta_row, visible=None):
    scale = key_rows.shape[1] ** (-0.5)
    scores_t = jnp.dot(key_rows, query_t, preferred_element_type=F32)
    weights_t = jnp.exp2(scores_t * (scale * LOG2E) - norm_row)
    if visible is not None:
        weights_t = jnp.where(visible, weights_t, jnp.zeros_like(weights_t))
    weight_grad_t = jnp.dot(value_rows, grad_t, preferred_element_type=F32)
    score_grad_t = (weights_t * (weight_grad_t - delta_row) * scale).astype(BF16)
    return weights_t.astype(BF16), score_grad_t


def suffix_kernel(
    info_ref, query_ref, out_ref, norm_ref, key_ref, value_ref, *refs
):
    grad_refs, refs = refs[:-10], refs[-10:]
    (
        query_rows_ref, grad_rows_ref, query_t_ref, grad_t_ref, norm_row_ref, delta_row_ref,
        query_acc_ref, key_grad_ref, value_grad_ref, grad_ref,
    ) = refs
    seq_len, width = key_ref.shape
    group_size = query_ref.shape[1] // width
    part = grad_refs[0].shape[0]
    for i, piece in enumerate(grad_refs):
        start = pl.multiple_of((info_ref[1] ^ i) * part, part)
        grad_ref[pl.ds(start, part), :] = piece[...]
    live_down = lax.broadcasted_iota(jnp.int32, (seq_len, width), 0) < info_ref[2]
    key_at = lax.broadcasted_iota(jnp.int32, (seq_len, seq_len), 0)
    query_at = lax.broadcasted_iota(jnp.int32, (seq_len, seq_len), 1)
    causal = key_at <= query_at
    key_rows, value_rows = key_ref[...], value_ref[...]
    key_t = key_rows.T
    key_acc = jnp.zeros((seq_len, width), F32)
    value_acc = jnp.zeros((seq_len, width), F32)
    for head in range(group_size):
        cols = slice(head * width, (head + 1) * width)
        rows = slice(head * seq_len, (head + 1) * seq_len)
        query_rows = query_ref[:, cols]
        grad_rows = grad_ref[:, cols]
        grad_rows = jnp.where(live_down, grad_rows, jnp.zeros_like(grad_rows))
        query_t, grad_t = query_rows.T, grad_rows.T
        out_t = out_ref[:, cols].T
        delta_row = jnp.sum(grad_t.astype(F32) * out_t.astype(F32), axis=0, keepdims=True)
        norm_row = norm_ref[head : head + 1, :] * LOG2E
        query_rows_ref[rows, :] = query_rows
        grad_rows_ref[rows, :] = grad_rows
        query_t_ref[:, rows] = query_t
        grad_t_ref[:, rows] = grad_t
        norm_row_ref[:, rows] = norm_row
        delta_row_ref[:, rows] = delta_row
        weights_t, score_grad_t = score_blocks(
            key_rows, value_rows, query_t, grad_t, norm_row, delta_row, causal
        )
        query_acc_ref[:, rows] = jnp.dot(key_t, score_grad_t, preferred_element_type=F32)
        key_acc += jnp.dot(score_grad_t, query_rows, preferred_element_type=F32)
        value_acc += jnp.dot(weights_t, grad_rows, preferred_element_type=F32)
    key_grad_ref[...] = key_acc.astype(BF16)
    value_grad_ref[...] = value_acc.astype(BF16)


def suffix_part(info, query, attn_out, log_norm, key_suffix, value_suffix, grads):
    seq_len, width = key_suffix.shape
    row_count = query.shape[0] * query.shape[1] // width
    shape = jax.ShapeDtypeStruct
    return pl.pallas_call(
        suffix_kernel,
        in_specs=[SMEM] + [VMEM] * (5 + len(grads)),
        out_specs=[VMEM] * 9,
        out_shape=[
            shape((row_count, width), BF16),
            shape((row_count, width), BF16),
            shape((width, row_count), BF16),
            shape((width, row_count), BF16),
            shape((1, row_count), F32),
            shape((1, row_count), F32),
            shape((width, row_count), F32),
            shape((seq_len, width), BF16),
            shape((seq_len, width), BF16),
        ],
        scratch_shapes=[pltpu.VMEM(query.shape, BF16)],
        compiler_params=PARAMS,
        cost_estimate=cost(row_count, seq_len, width),
        name="suffix_part",
    )(info, query, attn_out, log_norm, key_suffix, value_suffix, *grads)


def prompt_kernel(info_ref, *refs, blocks, count, last):
    pair_refs, refs = refs[:count], refs[count:]
    (
        query_rows_ref, grad_rows_ref, query_t_ref, grad_t_ref, norm_row_ref, delta_row_ref,
        query_acc_ref, query_grad_ref,
    ) = refs[:8]
    pair_grad_refs = refs[8:]
    chosen = info_ref[0]
    width = query_rows_ref.shape[1]

    def rows_of(which):
        parts = [ref[:, chosen, which] for ref in pair_refs]
        return jnp.concatenate([part.reshape(-1, width) for part in parts], 0)

    key_rows, value_rows = rows_of(0), rows_of(1)
    key_t = key_rows.T
    key_acc = jnp.zeros(key_rows.shape, F32)
    value_acc = jnp.zeros(key_rows.shape, F32)
    for head, rows in enumerate(blocks):
        weights_t, score_grad_t = score_blocks(
            key_rows, value_rows, query_t_ref[:, rows], grad_t_ref[:, rows],
            norm_row_ref[:, rows], delta_row_ref[:, rows],
        )
        query_part = jnp.dot(key_t, score_grad_t, preferred_element_type=F32)
        query_part += query_acc_ref[:, rows]
        if last:
            query_grad_ref[:, head * width : (head + 1) * width] = query_part.T.astype(BF16)
        else:
            query_grad_ref[:, rows] = query_part
        key_acc += jnp.dot(score_grad_t, query_rows_ref[rows, :], preferred_element_type=F32)
        value_acc += jnp.dot(weights_t, grad_rows_ref[rows, :], preferred_element_type=F32)
    size = key_rows.shape[0] // count
    key_grad, value_grad = key_acc.astype(BF16), value_acc.astype(BF16)
    mark = jnp.full((MARK, width), chosen.astype(F32), F32).astype(BF16)
    for i, ref in enumerate(pair_grad_refs):
        ref[:size] = key_grad[i * size : (i + 1) * size]
        ref[size : 2 * size] = value_grad[i * size : (i + 1) * size]
        ref[2 * size :] = mark


def prompt_part(info, pairs, rows, query_acc, seq_len, last=False):
    row_count, width = rows[0].shape
    blocks = [slice(at, at + seq_len) for at in range(0, row_count, seq_len)]
    stacks, _, _, owned, _ = pairs[0].shape
    size = stacks * owned
    out = jax.ShapeDtypeStruct((width, row_count), F32)
    if last:
        out = jax.ShapeDtypeStruct((seq_len, row_count * width // seq_len), BF16)
    pair_out = jax.ShapeDtypeStruct((2 * size + MARK, width), BF16)
    return pl.pallas_call(
        functools.partial(prompt_kernel, blocks=blocks, count=len(pairs), last=last),
        in_specs=[SMEM] + [VMEM] * (len(pairs) + 7),
        out_specs=[VMEM] * (1 + len(pairs)),
        out_shape=[out] + [pair_out] * len(pairs),
        compiler_params=PARAMS,
        cost_estimate=cost(row_count, len(pairs) * size, width),
        name="prompt_part",
    )(info, *pairs, *rows, query_acc)


def group_kernel(*refs):
    share_refs, total_ref = refs[:-1], refs[-1]
    stacks, prompt_count, _, owned, width = total_ref.shape
    size = stacks * owned
    for which in range(2):
        rows = slice(which * size, (which + 1) * size)
        totals = [jnp.zeros((size, width), F32)] * prompt_count
        for ref in share_refs:
            share = ref[rows].astype(F32)
            mark = ref[2 * size :].astype(F32)[:1]
            for i in range(prompt_count):
                totals[i] += jnp.where(mark == float(i), share, 0.0)
        for i in range(prompt_count):
            total_ref[:, i, which] = totals[i].astype(BF16).reshape(stacks, owned, width)


def group_sum(shares, shape):
    return pl.pallas_call(
        group_kernel,
        in_specs=[VMEM] * len(shares),
        out_specs=VMEM,
        out_shape=jax.ShapeDtypeStruct(shape, BF16),
        compiler_params=PARAMS,
        name="group_sum",
    )(*shares)


def exchange(blocks, axes):
    return lax.all_to_all(blocks, axes, split_axis=0, concat_axis=0, tiled=True)


def trade(block, axis, target):
    return lax.ppermute(block, axis, [(i, target(i)) for i in range(lax.axis_size(axis))])


def copies(block, count):
    return jnp.broadcast_to(block[None], (count,) + block.shape)


def per_device(
    query, key_suffix, value_suffix, key_prompt, value_prompt, attn_out, grad_out, log_norm,
    prompt_id, lengths,
):
    seq_len, columns = query.shape[1:]
    width = key_suffix.shape[2]
    prompt_count, owned = key_prompt.shape[:2]
    heads, stacks, lines = lax.axis_size("head"), lax.axis_size("z"), lax.axis_size("y")
    place = lax.axis_index("head")
    info = jnp.stack([prompt_id[0], place, lengths[0]]).astype(jnp.int32)

    own_pair = jnp.stack([key_prompt, value_prompt], 1).reshape(-1, width)
    stacked = exchange(copies(own_pair, stacks).reshape(-1, width), "z")
    grads = []
    for i in range(heads):
        at = (place ^ i) * columns
        piece = lax.dynamic_slice_in_dim(grad_out[0], at, columns, axis=1)
        grads.append(trade(piece, "head", lambda j, i=i: j ^ i) if i else piece)
    stacked, info, *grads = lax.optimization_barrier((stacked, info, *grads))
    stacked = stacked.reshape(stacks, prompt_count, 2, owned, width)

    moved = {
        steps: trade(stacked, "y", lambda j, steps=steps: (j + steps) % lines)
        for steps in (1, lines - 1, 2)
    }
    *rows, query_acc, key_grad, value_grad = suffix_part(
        info, query[0], attn_out[0], log_norm[0], key_suffix[0], value_suffix[0], grads
    )
    near, key_grad = lax.optimization_barrier(([stacked, moved[1], moved[lines - 1]], key_grad))
    near_other = [trade(block, "c", lambda j: j ^ 1) for block in near]

    shares = []

    def send(parts, places):
        for part, (steps, other) in zip(parts, places, strict=True):
            if not steps and not other:
                shares.append(part)
                continue
            target = lambda j, s=steps, o=other: 2 * ((j // 2 - s) % lines) + (j % 2 ^ o)
            shares.append(trade(part, GROUP, target))

    query_acc, *parts = prompt_part(info, near, rows, query_acc, seq_len)
    far, query_acc = lax.optimization_barrier((moved[2], query_acc))
    far_other = trade(far, "c", lambda j: j ^ 1)
    send(parts, [(0, 0), (1, 0), (lines - 1, 0)])
    query_acc, *parts = prompt_part(info, [far, far_other], rows, query_acc, seq_len)
    send(parts, [(2, 0), (2, 1)])
    query_acc, near_other, shares[:3] = lax.optimization_barrier(
        (query_acc, near_other, shares[:3])
    )
    query_grad, *parts = prompt_part(info, near_other, rows, query_acc, seq_len, True)
    parts, shares[3:] = lax.optimization_barrier((parts, shares[3:]))
    send(parts, [(0, 1), (1, 1), (lines - 1, 1)])

    totals = group_sum(shares, (stacks, prompt_count, 2, owned, width))
    final = exchange(totals.reshape(-1, prompt_count * 2 * owned, width), "z")
    final = jnp.sum(final.astype(F32), 0).astype(BF16)
    final = final.reshape(prompt_count, 2, owned, width)
    return (query_grad[None], key_grad[None], value_grad[None], final[:, 0], final[:, 1])


def solution(mesh):
    roll, head = mesh.devices.shape
    fine = Mesh(mesh.devices.reshape(roll // 8, 4, 2, head), ("z", "y", "c", "head"))
    rolls = ("z", "y", "c")
    by_rollout = P(rolls, None, "head")
    by_key = P(None, rolls, "head")
    by_row = P(rolls, "head", None)
    in_specs = (
        by_rollout, by_rollout, by_rollout, by_key, by_key, by_rollout, by_row, by_row,
        P(rolls), P(rolls),
    )
    out_specs = (by_rollout, by_rollout, by_rollout, by_key, by_key)
    return jax.shard_map(
        per_device, mesh=fine, in_specs=in_specs, out_specs=out_specs, check_vma=False
    )
```

```python
import functools

import jax
import jax.numpy as jnp
from jax import lax
from jax.experimental import pallas as pl
from jax.experimental.pallas import tpu as pltpu
from jax.sharding import Mesh
from jax.sharding import PartitionSpec as P

BF16 = jnp.bfloat16
F32 = jnp.float32
GROUP = ("y", "c")
LOG2E = 1.4426950408889634
VMEM = pl.BlockSpec(memory_space=pltpu.VMEM)
SMEM = pl.BlockSpec(memory_space=pltpu.SMEM)
PARAMS = pltpu.CompilerParams(vmem_limit_bytes=28 * 1024 * 1024)
MARK = 16


def cost(row_count, key_count, width):
    pairs = row_count * key_count
    return pl.CostEstimate(
        flops=10 * pairs * width, bytes_accessed=16 * row_count * width, transcendentals=pairs
    )


def score_blocks(key_rows, value_rows, query_t, grad_t, norm_row, delta_row, visible=None):
    scale = key_rows.shape[1] ** (-0.5)
    scores_t = jnp.dot(key_rows, query_t, preferred_element_type=F32)
    weights_t = jnp.exp2(scores_t * (scale * LOG2E) - norm_row)
    if visible is not None:
        weights_t = jnp.where(visible, weights_t, jnp.zeros_like(weights_t))
    weight_grad_t = jnp.dot(value_rows, grad_t, preferred_element_type=F32)
    score_grad_t = (weights_t * (weight_grad_t - delta_row) * scale).astype(BF16)
    return weights_t.astype(BF16), score_grad_t


def suffix_kernel(
    info_ref, query_ref, out_ref, norm_ref, key_ref, value_ref, *refs
):
    grad_refs, refs = refs[:-10], refs[-10:]
    (
        query_rows_ref, grad_rows_ref, query_t_ref, grad_t_ref, norm_row_ref, delta_row_ref,
        query_acc_ref, key_grad_ref, value_grad_ref, grad_ref,
    ) = refs
    seq_len, width = key_ref.shape
    group_size = query_ref.shape[1] // width
    part = grad_refs[0].shape[0]
    for i, piece in enumerate(grad_refs):
        start = pl.multiple_of((info_ref[1] ^ i) * part, part)
        grad_ref[pl.ds(start, part), :] = piece[...]
    live_down = lax.broadcasted_iota(jnp.int32, (seq_len, width), 0) < info_ref[2]
    key_at = lax.broadcasted_iota(jnp.int32, (seq_len, seq_len), 0)
    query_at = lax.broadcasted_iota(jnp.int32, (seq_len, seq_len), 1)
    causal = key_at <= query_at
    key_rows, value_rows = key_ref[...], value_ref[...]
    key_t = key_rows.T
    key_acc = jnp.zeros((seq_len, width), F32)
    value_acc = jnp.zeros((seq_len, width), F32)
    for head in range(group_size):
        cols = slice(head * width, (head + 1) * width)
        rows = slice(head * seq_len, (head + 1) * seq_len)
        query_rows = query_ref[:, cols]
        grad_rows = grad_ref[:, cols]
        grad_rows = jnp.where(live_down, grad_rows, jnp.zeros_like(grad_rows))
        query_t, grad_t = query_rows.T, grad_rows.T
        out_t = out_ref[:, cols].T
        delta_row = jnp.sum(grad_t.astype(F32) * out_t.astype(F32), axis=0, keepdims=True)
        norm_row = norm_ref[head : head + 1, :] * LOG2E
        query_rows_ref[rows, :] = query_rows
        grad_rows_ref[rows, :] = grad_rows
        query_t_ref[:, rows] = query_t
        grad_t_ref[:, rows] = grad_t
        norm_row_ref[:, rows] = norm_row
        delta_row_ref[:, rows] = delta_row
        weights_t, score_grad_t = score_blocks(
            key_rows, value_rows, query_t, grad_t, norm_row, delta_row, causal
        )
        query_acc_ref[:, rows] = jnp.dot(key_t, score_grad_t, preferred_element_type=F32)
        key_acc += jnp.dot(score_grad_t, query_rows, preferred_element_type=F32)
        value_acc += jnp.dot(weights_t, grad_rows, preferred_element_type=F32)
    key_grad_ref[...] = key_acc.astype(BF16)
    value_grad_ref[...] = value_acc.astype(BF16)


def suffix_part(info, query, attn_out, log_norm, key_suffix, value_suffix, grads):
    seq_len, width = key_suffix.shape
    row_count = query.shape[0] * query.shape[1] // width
    shape = jax.ShapeDtypeStruct
    return pl.pallas_call(
        suffix_kernel,
        in_specs=[SMEM] + [VMEM] * (5 + len(grads)),
        out_specs=[VMEM] * 9,
        out_shape=[
            shape((row_count, width), BF16),
            shape((row_count, width), BF16),
            shape((width, row_count), BF16),
            shape((width, row_count), BF16),
            shape((1, row_count), F32),
            shape((1, row_count), F32),
            shape((width, row_count), F32),
            shape((seq_len, width), BF16),
            shape((seq_len, width), BF16),
        ],
        scratch_shapes=[pltpu.VMEM(query.shape, BF16)],
        compiler_params=PARAMS,
        cost_estimate=cost(row_count, seq_len, width),
        name="suffix_part",
    )(info, query, attn_out, log_norm, key_suffix, value_suffix, *grads)


def prompt_kernel(info_ref, *refs, blocks, count, last):
    pair_refs, refs = refs[:count], refs[count:]
    (
        query_rows_ref, grad_rows_ref, query_t_ref, grad_t_ref, norm_row_ref, delta_row_ref,
        query_acc_ref, query_grad_ref,
    ) = refs[:8]
    pair_grad_refs = refs[8:]
    chosen = info_ref[0]
    width = query_rows_ref.shape[1]

    def rows_of(which):
        parts = [ref[:, chosen, which] for ref in pair_refs]
        return jnp.concatenate([part.reshape(-1, width) for part in parts], 0)

    key_rows, value_rows = rows_of(0), rows_of(1)
    key_t = key_rows.T
    key_acc = jnp.zeros(key_rows.shape, F32)
    value_acc = jnp.zeros(key_rows.shape, F32)
    for head, rows in enumerate(blocks):
        weights_t, score_grad_t = score_blocks(
            key_rows, value_rows, query_t_ref[:, rows], grad_t_ref[:, rows],
            norm_row_ref[:, rows], delta_row_ref[:, rows],
        )
        query_part = jnp.dot(key_t, score_grad_t, preferred_element_type=F32)
        query_part += query_acc_ref[:, rows]
        if last:
            query_grad_ref[:, head * width : (head + 1) * width] = query_part.T.astype(BF16)
        else:
            query_grad_ref[:, rows] = query_part
        key_acc += jnp.dot(score_grad_t, query_rows_ref[rows, :], preferred_element_type=F32)
        value_acc += jnp.dot(weights_t, grad_rows_ref[rows, :], preferred_element_type=F32)
    size = key_rows.shape[0] // count
    key_grad, value_grad = key_acc.astype(BF16), value_acc.astype(BF16)
    mark = jnp.full((MARK, width), chosen.astype(F32), F32).astype(BF16)
    for i, ref in enumerate(pair_grad_refs):
        ref[:size] = key_grad[i * size : (i + 1) * size]
        ref[size : 2 * size] = value_grad[i * size : (i + 1) * size]
        ref[2 * size :] = mark


def prompt_part(info, pairs, rows, query_acc, seq_len, last=False):
    row_count, width = rows[0].shape
    blocks = [slice(at, at + seq_len) for at in range(0, row_count, seq_len)]
    stacks, _, _, owned, _ = pairs[0].shape
    size = stacks * owned
    out = jax.ShapeDtypeStruct((width, row_count), F32)
    if last:
        out = jax.ShapeDtypeStruct((seq_len, row_count * width // seq_len), BF16)
    pair_out = jax.ShapeDtypeStruct((2 * size + MARK, width), BF16)
    return pl.pallas_call(
        functools.partial(prompt_kernel, blocks=blocks, count=len(pairs), last=last),
        in_specs=[SMEM] + [VMEM] * (len(pairs) + 7),
        out_specs=[VMEM] * (1 + len(pairs)),
        out_shape=[out] + [pair_out] * len(pairs),
        compiler_params=PARAMS,
        cost_estimate=cost(row_count, len(pairs) * size, width),
        name="prompt_part",
    )(info, *pairs, *rows, query_acc)


def group_kernel(*refs):
    share_refs, total_ref = refs[:-1], refs[-1]
    stacks, prompt_count, _, owned, width = total_ref.shape
    size = stacks * owned
    for which in range(2):
        rows = slice(which * size, (which + 1) * size)
        totals = [jnp.zeros((size, width), F32)] * prompt_count
        for ref in share_refs:
            share = ref[rows].astype(F32)
            mark = ref[2 * size :].astype(F32)[:1]
            for i in range(prompt_count):
                totals[i] += jnp.where(mark == float(i), share, 0.0)
        for i in range(prompt_count):
            total_ref[:, i, which] = totals[i].astype(BF16).reshape(stacks, owned, width)


def group_sum(shares, shape):
    return pl.pallas_call(
        group_kernel,
        in_specs=[VMEM] * len(shares),
        out_specs=VMEM,
        out_shape=jax.ShapeDtypeStruct(shape, BF16),
        compiler_params=PARAMS,
        name="group_sum",
    )(*shares)


def exchange(blocks, axes):
    return lax.all_to_all(blocks, axes, split_axis=0, concat_axis=0, tiled=True)


def trade(block, axis, target):
    return lax.ppermute(block, axis, [(i, target(i)) for i in range(lax.axis_size(axis))])


def copies(block, count):
    return jnp.broadcast_to(block[None], (count,) + block.shape)


def per_device(
    query, key_suffix, value_suffix, key_prompt, value_prompt, attn_out, grad_out, log_norm,
    prompt_id, lengths,
):
    seq_len, columns = query.shape[1:]
    width = key_suffix.shape[2]
    prompt_count, owned = key_prompt.shape[:2]
    heads, stacks, lines = lax.axis_size("head"), lax.axis_size("z"), lax.axis_size("y")
    place = lax.axis_index("head")
    info = jnp.stack([prompt_id[0], place, lengths[0]]).astype(jnp.int32)

    own_pair = jnp.stack([key_prompt, value_prompt], 1).reshape(-1, width)
    stacked = exchange(copies(own_pair, stacks).reshape(-1, width), "z")
    grads = []
    for i in range(heads):
        at = (place ^ i) * columns
        piece = lax.dynamic_slice_in_dim(grad_out[0], at, columns, axis=1)
        grads.append(trade(piece, "head", lambda j, i=i: j ^ i) if i else piece)
    stacked, info = lax.optimization_barrier((stacked, info))
    stacked = stacked.reshape(stacks, prompt_count, 2, owned, width)

    moved = {
        steps: trade(stacked, "y", lambda j, steps=steps: (j + steps) % lines)
        for steps in (1, lines - 1, 2)
    }
    *rows, query_acc, key_grad, value_grad = suffix_part(
        info, query[0], attn_out[0], log_norm[0], key_suffix[0], value_suffix[0], grads
    )
    near, key_grad = lax.optimization_barrier(([stacked, moved[1], moved[lines - 1]], key_grad))
    near_other = [trade(block, "c", lambda j: j ^ 1) for block in near]

    shares = []

    def send(parts, places):
        for part, (steps, other) in zip(parts, places, strict=True):
            if not steps and not other:
                shares.append(part)
                continue
            target = lambda j, s=steps, o=other: 2 * ((j // 2 - s) % lines) + (j % 2 ^ o)
            shares.append(trade(part, GROUP, target))

    query_acc, *parts = prompt_part(info, near, rows, query_acc, seq_len)
    far, query_acc = lax.optimization_barrier((moved[2], query_acc))
    far_other = trade(far, "c", lambda j: j ^ 1)
    send(parts, [(0, 0), (1, 0), (lines - 1, 0)])
    query_acc, *parts = prompt_part(info, [far, far_other], rows, query_acc, seq_len)
    send(parts, [(2, 0), (2, 1)])
    query_acc, near_other, shares[:3] = lax.optimization_barrier(
        (query_acc, near_other, shares[:3])
    )
    query_grad, *parts = prompt_part(info, near_other, rows, query_acc, seq_len, True)
    parts, shares[3:] = lax.optimization_barrier((parts, shares[3:]))
    send(parts, [(0, 1), (1, 1), (lines - 1, 1)])

    totals = group_sum(shares, (stacks, prompt_count, 2, owned, width))
    final = exchange(totals.reshape(-1, prompt_count * 2 * owned, width), "z")
    final = jnp.sum(final.astype(F32), 0).astype(BF16)
    final = final.reshape(prompt_count, 2, owned, width)
    return (query_grad[None], key_grad[None], value_grad[None], final[:, 0], final[:, 1])


def solution(mesh):
    roll, head = mesh.devices.shape
    fine = Mesh(mesh.devices.reshape(roll // 8, 4, 2, head), ("z", "y", "c", "head"))
    rolls = ("z", "y", "c")
    by_rollout = P(rolls, None, "head")
    by_key = P(None, rolls, "head")
    by_row = P(rolls, "head", None)
    in_specs = (
        by_rollout, by_rollout, by_rollout, by_key, by_key, by_rollout, by_row, by_row,
        P(rolls), P(rolls),
    )
    out_specs = (by_rollout, by_rollout, by_rollout, by_key, by_key)
    return jax.shard_map(
        per_device, mesh=fine, in_specs=in_specs, out_specs=out_specs, check_vma=False
    )
```

```python
import functools

import jax
import jax.numpy as jnp
from jax import lax
from jax.experimental import pallas as pl
from jax.experimental.pallas import tpu as pltpu
from jax.sharding import Mesh
from jax.sharding import PartitionSpec as P

BF16 = jnp.bfloat16
F32 = jnp.float32
GROUP = ("y", "c")
LOG2E = 1.4426950408889634
VMEM = pl.BlockSpec(memory_space=pltpu.VMEM)
SMEM = pl.BlockSpec(memory_space=pltpu.SMEM)
PARAMS = pltpu.CompilerParams(vmem_limit_bytes=28 * 1024 * 1024)
MARK = 16


def cost(row_count, key_count, width):
    pairs = row_count * key_count
    return pl.CostEstimate(
        flops=10 * pairs * width, bytes_accessed=16 * row_count * width, transcendentals=pairs
    )


def score_blocks(key_rows, value_rows, query_t, grad_t, norm_row, delta_row, visible=None):
    scale = key_rows.shape[1] ** (-0.5)
    scores_t = jnp.dot(key_rows, query_t, preferred_element_type=F32)
    weights_t = jnp.exp2(scores_t * (scale * LOG2E) - norm_row)
    if visible is not None:
        weights_t = jnp.where(visible, weights_t, jnp.zeros_like(weights_t))
    weight_grad_t = jnp.dot(value_rows, grad_t, preferred_element_type=F32)
    score_grad_t = (weights_t * (weight_grad_t - delta_row) * scale).astype(BF16)
    return weights_t.astype(BF16), score_grad_t


def prepare_kernel(info_ref, query_ref, out_ref, norm_ref, *refs):
    grad_refs, refs = refs[:-5], refs[-5:]
    grad_rows_ref, query_t_ref, grad_t_ref, norm_row_ref, delta_row_ref = refs
    group_size, seq_len = norm_ref.shape
    width = query_ref.shape[1] // group_size
    part = grad_refs[0].shape[0]
    at = lax.broadcasted_iota(jnp.int32, grad_refs[0].shape, 0)
    for i, piece in enumerate(grad_refs):
        start = pl.multiple_of((info_ref[1] ^ i) * part, part)
        rows = piece[...]
        rows = jnp.where(at + start < info_ref[2], rows, jnp.zeros_like(rows))
        grad_rows_ref[pl.ds(start, part), :] = rows
    for head in range(group_size):
        cols = slice(head * width, (head + 1) * width)
        rows = slice(head * seq_len, (head + 1) * seq_len)
        grad_t = grad_rows_ref[:, cols].T
        out_t = out_ref[:, cols].T
        query_t_ref[:, rows] = query_ref[:, cols].T
        grad_t_ref[:, rows] = grad_t
        norm_row_ref[:, rows] = norm_ref[head : head + 1, :] * LOG2E
        delta_row_ref[:, rows] = jnp.sum(
            grad_t.astype(F32) * out_t.astype(F32), axis=0, keepdims=True
        )


def prepare(info, query, attn_out, log_norm, grads):
    group_size, seq_len = log_norm.shape
    width = query.shape[1] // group_size
    row_count = group_size * seq_len
    shape = jax.ShapeDtypeStruct
    return pl.pallas_call(
        prepare_kernel,
        in_specs=[SMEM] + [VMEM] * (3 + len(grads)),
        out_specs=[VMEM] * 5,
        out_shape=[
            shape(query.shape, BF16),
            shape((width, row_count), BF16),
            shape((width, row_count), BF16),
            shape((1, row_count), F32),
            shape((1, row_count), F32),
        ],
        compiler_params=PARAMS,
        cost_estimate=pl.CostEstimate(
            flops=2 * row_count * width, bytes_accessed=12 * row_count * width, transcendentals=0
        ),
        name="prepare",
    )(info, query, attn_out, log_norm, *grads)


def attend_head(head, row_refs, key_rows, value_rows, key_t, visible=None):
    query_ref, grad_rows_ref, query_t_ref, grad_t_ref, norm_row_ref, delta_row_ref = row_refs
    width = key_rows.shape[1]
    seq_len = query_ref.shape[0]
    cols = slice(head * width, (head + 1) * width)
    rows = slice(head * seq_len, (head + 1) * seq_len)
    weights_t, score_grad_t = score_blocks(
        key_rows, value_rows, query_t_ref[:, rows], grad_t_ref[:, rows],
        norm_row_ref[:, rows], delta_row_ref[:, rows], visible,
    )
    query_part = jnp.dot(key_t, score_grad_t, preferred_element_type=F32)
    key_part = jnp.dot(score_grad_t, query_ref[:, cols], preferred_element_type=F32)
    value_part = jnp.dot(weights_t, grad_rows_ref[:, cols], preferred_element_type=F32)
    return rows, cols, query_part, key_part, value_part


def suffix_kernel(*refs):
    row_refs, refs = refs[:6], refs[6:]
    query_acc_ref, key_ref, value_ref, query_grad_ref, key_grad_ref, value_grad_ref = refs
    seq_len, width = key_ref.shape
    key_at = lax.broadcasted_iota(jnp.int32, (seq_len, seq_len), 0)
    query_at = lax.broadcasted_iota(jnp.int32, (seq_len, seq_len), 1)
    causal = key_at <= query_at
    key_rows, value_rows = key_ref[...], value_ref[...]
    key_t = key_rows.T
    key_acc = jnp.zeros((seq_len, width), F32)
    value_acc = jnp.zeros((seq_len, width), F32)
    for head in range(query_grad_ref.shape[1] // width):
        rows, cols, query_part, key_part, value_part = attend_head(
            head, row_refs, key_rows, value_rows, key_t, causal
        )
        query_grad_ref[:, cols] = (query_part + query_acc_ref[:, rows]).T.astype(BF16)
        key_acc += key_part
        value_acc += value_part
    key_grad_ref[...] = key_acc.astype(BF16)
    value_grad_ref[...] = value_acc.astype(BF16)


def suffix_part(rows, query_acc, key_suffix, value_suffix):
    seq_len, width = key_suffix.shape
    suffix = jax.ShapeDtypeStruct(key_suffix.shape, BF16)
    return pl.pallas_call(
        suffix_kernel,
        in_specs=[VMEM] * (len(rows) + 3),
        out_specs=[VMEM] * 3,
        out_shape=[jax.ShapeDtypeStruct(rows[0].shape, BF16), suffix, suffix],
        compiler_params=PARAMS,
        cost_estimate=cost(query_acc.shape[1], seq_len, width),
        name="suffix_part",
    )(*rows, query_acc, key_suffix, value_suffix)


def prompt_kernel(info_ref, *refs, count, first):
    pair_refs, row_refs, refs = refs[:count], refs[count : count + 6], refs[count + 6 :]
    query_acc_ref = None if first else refs[0]
    query_out_ref, *pair_grad_refs = refs if first else refs[1:]
    chosen = info_ref[0]
    width = query_out_ref.shape[0]

    def rows_of(which):
        parts = [ref[:, chosen, which] for ref in pair_refs]
        return jnp.concatenate([part.reshape(-1, width) for part in parts], 0)

    key_rows, value_rows = rows_of(0), rows_of(1)
    key_t = key_rows.T
    key_acc = jnp.zeros(key_rows.shape, F32)
    value_acc = jnp.zeros(key_rows.shape, F32)
    for head in range(row_refs[0].shape[1] // width):
        rows, _, query_part, key_part, value_part = attend_head(
            head, row_refs, key_rows, value_rows, key_t
        )
        query_out_ref[:, rows] = query_part if first else query_part + query_acc_ref[:, rows]
        key_acc += key_part
        value_acc += value_part
    size = key_rows.shape[0] // count
    key_grad, value_grad = key_acc.astype(BF16), value_acc.astype(BF16)
    mark = jnp.full((MARK, width), chosen.astype(F32), F32).astype(BF16)
    for i, ref in enumerate(pair_grad_refs):
        ref[:size] = key_grad[i * size : (i + 1) * size]
        ref[size : 2 * size] = value_grad[i * size : (i + 1) * size]
        ref[2 * size :] = mark


def prompt_part(info, pairs, rows, query_acc=None):
    width, row_count = rows[2].shape
    stacks, _, _, owned, _ = pairs[0].shape
    size = stacks * owned
    out = jax.ShapeDtypeStruct((width, row_count), F32)
    pair_out = jax.ShapeDtypeStruct((2 * size + MARK, width), BF16)
    more = [] if query_acc is None else [query_acc]
    return pl.pallas_call(
        functools.partial(prompt_kernel, count=len(pairs), first=query_acc is None),
        in_specs=[SMEM] + [VMEM] * (len(pairs) + len(rows) + len(more)),
        out_specs=[VMEM] * (1 + len(pairs)),
        out_shape=[out] + [pair_out] * len(pairs),
        compiler_params=PARAMS,
        cost_estimate=cost(row_count, len(pairs) * size, width),
        name="prompt_part",
    )(info, *pairs, *rows, *more)


def group_kernel(*refs):
    share_refs, total_ref = refs[:-1], refs[-1]
    stacks, prompt_count, _, owned, width = total_ref.shape
    size = stacks * owned
    for which in range(2):
        rows = slice(which * size, (which + 1) * size)
        totals = [jnp.zeros((size, width), F32)] * prompt_count
        for ref in share_refs:
            share = ref[rows].astype(F32)
            mark = ref[2 * size :].astype(F32)[:1]
            for i in range(prompt_count):
                totals[i] += jnp.where(mark == float(i), share, 0.0)
        for i in range(prompt_count):
            total_ref[:, i, which] = totals[i].astype(BF16).reshape(stacks, owned, width)


def group_sum(shares, shape):
    return pl.pallas_call(
        group_kernel,
        in_specs=[VMEM] * len(shares),
        out_specs=VMEM,
        out_shape=jax.ShapeDtypeStruct(shape, BF16),
        compiler_params=PARAMS,
        name="group_sum",
    )(*shares)


def exchange(blocks, axes):
    return lax.all_to_all(blocks, axes, split_axis=0, concat_axis=0, tiled=True)


def trade(block, axis, target):
    return lax.ppermute(block, axis, [(i, target(i)) for i in range(lax.axis_size(axis))])


def copies(block, count):
    return jnp.broadcast_to(block[None], (count,) + block.shape)


def per_device(
    query, key_suffix, value_suffix, key_prompt, value_prompt, attn_out, grad_out, log_norm,
    prompt_id, lengths,
):
    columns = query.shape[2]
    width = key_suffix.shape[2]
    prompt_count, owned = key_prompt.shape[:2]
    heads, stacks, lines = lax.axis_size("head"), lax.axis_size("z"), lax.axis_size("y")
    place = lax.axis_index("head")
    info = jnp.stack([prompt_id[0], place, lengths[0]]).astype(jnp.int32)

    own_pair = jnp.stack([key_prompt, value_prompt], 1).reshape(-1, width)
    stacked = exchange(copies(own_pair, stacks).reshape(-1, width), "z")
    grads = []
    for i in range(heads):
        at = (place ^ i) * columns
        piece = lax.dynamic_slice_in_dim(grad_out[0], at, columns, axis=1)
        grads.append(trade(piece, "head", lambda j, i=i: j ^ i) if i else piece)
    stacked, info = lax.optimization_barrier((stacked, info))
    stacked = stacked.reshape(stacks, prompt_count, 2, owned, width)

    moved = {
        steps: trade(stacked, "y", lambda j, steps=steps: (j + steps) % lines)
        for steps in (1, lines - 1, 2)
    }
    stacked, grads = lax.optimization_barrier((stacked, grads))
    other = trade(stacked, "c", lambda j: j ^ 1)
    rows = [query[0], *prepare(info, query[0], attn_out[0], log_norm[0], grads)]
    beside, rows[-1] = lax.optimization_barrier(([moved[1], moved[lines - 1]], rows[-1]))
    beside_other = [trade(block, "c", lambda j: j ^ 1) for block in beside]

    shares = []

    def send(parts, places):
        for part, (steps, across) in zip(parts, places, strict=True):
            if not steps and not across:
                shares.append(part)
                continue
            target = lambda j, s=steps, o=across: 2 * ((j // 2 - s) % lines) + (j % 2 ^ o)
            shares.append(trade(part, GROUP, target))

    query_acc, *parts = prompt_part(info, [stacked, *beside, other], rows)
    far, query_acc = lax.optimization_barrier((moved[2], query_acc))
    far_other = trade(far, "c", lambda j: j ^ 1)
    send(parts, [(0, 0), (1, 0), (lines - 1, 0), (0, 1)])
    query_acc, *parts = prompt_part(info, [*beside_other, far, far_other], rows, query_acc)
    parts, shares = lax.optimization_barrier((parts, shares))
    send(parts, [(1, 1), (lines - 1, 1), (2, 0), (2, 1)])

    query_grad, key_grad, value_grad = suffix_part(rows, query_acc, key_suffix[0], value_suffix[0])
    key_grad, shares = lax.optimization_barrier((key_grad, shares))

    totals = group_sum(shares, (stacks, prompt_count, 2, owned, width))
    final = exchange(totals.reshape(-1, prompt_count * 2 * owned, width), "z")
    final = jnp.sum(final.astype(F32), 0).astype(BF16)
    final = final.reshape(prompt_count, 2, owned, width)
    return (query_grad[None], key_grad[None], value_grad[None], final[:, 0], final[:, 1])


def solution(mesh):
    roll, head = mesh.devices.shape
    fine = Mesh(mesh.devices.reshape(roll // 8, 4, 2, head), ("z", "y", "c", "head"))
    rolls = ("z", "y", "c")
    by_rollout = P(rolls, None, "head")
    by_key = P(None, rolls, "head")
    by_row = P(rolls, "head", None)
    in_specs = (
        by_rollout, by_rollout, by_rollout, by_key, by_key, by_rollout, by_row, by_row,
        P(rolls), P(rolls),
    )
    out_specs = (by_rollout, by_rollout, by_rollout, by_key, by_key)
    return jax.shard_map(
        per_device, mesh=fine, in_specs=in_specs, out_specs=out_specs, check_vma=False
    )
```

```python
import functools

import jax
import jax.numpy as jnp
from jax import lax
from jax.experimental import pallas as pl
from jax.experimental.pallas import tpu as pltpu
from jax.sharding import Mesh
from jax.sharding import PartitionSpec as P

BF16 = jnp.bfloat16
F32 = jnp.float32
GROUP = ("y", "c")
LOG2E = 1.4426950408889634
VMEM = pl.BlockSpec(memory_space=pltpu.VMEM)
SMEM = pl.BlockSpec(memory_space=pltpu.SMEM)
PARAMS = pltpu.CompilerParams(vmem_limit_bytes=28 * 1024 * 1024)
MARK = 16


def cost(row_count, key_count, width):
    pairs = row_count * key_count
    return pl.CostEstimate(
        flops=10 * pairs * width, bytes_accessed=16 * row_count * width, transcendentals=pairs
    )


def score_blocks(key_rows, value_rows, query_t, grad_t, norm_row, delta_row, visible=None):
    scale = key_rows.shape[1] ** (-0.5)
    scores_t = jnp.dot(key_rows, query_t, preferred_element_type=F32)
    weights_t = jnp.exp2(scores_t * (scale * LOG2E) - norm_row)
    if visible is not None:
        weights_t = jnp.where(visible, weights_t, jnp.zeros_like(weights_t))
    weight_grad_t = jnp.dot(value_rows, grad_t, preferred_element_type=F32)
    score_grad_t = (weights_t * (weight_grad_t - delta_row) * scale).astype(BF16)
    return weights_t.astype(BF16), score_grad_t


def spread_kernel(key_ref, value_ref, out_ref):
    for i in range(out_ref.shape[0]):
        out_ref[i, :, 0] = key_ref[...]
        out_ref[i, :, 1] = value_ref[...]


def spread(keys, values, count):
    prompt_count, owned, width = keys.shape
    return pl.pallas_call(
        spread_kernel,
        in_specs=[VMEM] * 2,
        out_specs=VMEM,
        out_shape=jax.ShapeDtypeStruct((count, prompt_count, 2, owned, width), BF16),
        name="spread",
    )(keys, values)


def prepare_kernel(info_ref, query_ref, out_ref, norm_ref, *refs):
    grad_refs, refs = refs[:-5], refs[-5:]
    grad_rows_ref, query_t_ref, grad_t_ref, norm_row_ref, delta_row_ref = refs
    group_size, seq_len = norm_ref.shape
    width = query_ref.shape[1] // group_size
    part = grad_refs[0].shape[0]
    at = lax.broadcasted_iota(jnp.int32, grad_refs[0].shape, 0)
    for i, piece in enumerate(grad_refs):
        start = pl.multiple_of((info_ref[1] ^ i) * part, part)
        rows = piece[...]
        rows = jnp.where(at + start < info_ref[2], rows, jnp.zeros_like(rows))
        grad_rows_ref[pl.ds(start, part), :] = rows
    for head in range(group_size):
        cols = slice(head * width, (head + 1) * width)
        rows = slice(head * seq_len, (head + 1) * seq_len)
        grad_t = grad_rows_ref[:, cols].T
        out_t = out_ref[:, cols].T
        query_t_ref[:, rows] = query_ref[:, cols].T
        grad_t_ref[:, rows] = grad_t
        norm_row_ref[:, rows] = norm_ref[head : head + 1, :] * LOG2E
        delta_row_ref[:, rows] = jnp.sum(
            grad_t.astype(F32) * out_t.astype(F32), axis=0, keepdims=True
        )


def prepare(info, query, attn_out, log_norm, grads):
    group_size, seq_len = log_norm.shape
    width = query.shape[1] // group_size
    row_count = group_size * seq_len
    shape = jax.ShapeDtypeStruct
    return pl.pallas_call(
        prepare_kernel,
        in_specs=[SMEM] + [VMEM] * (3 + len(grads)),
        out_specs=[VMEM] * 5,
        out_shape=[
            shape(query.shape, BF16),
            shape((width, row_count), BF16),
            shape((width, row_count), BF16),
            shape((1, row_count), F32),
            shape((1, row_count), F32),
        ],
        compiler_params=PARAMS,
        cost_estimate=pl.CostEstimate(
            flops=2 * row_count * width, bytes_accessed=12 * row_count * width, transcendentals=0
        ),
        name="prepare",
    )(info, query, attn_out, log_norm, *grads)


def attend_head(head, row_refs, key_rows, value_rows, key_t, visible=None):
    query_ref, grad_rows_ref, query_t_ref, grad_t_ref, norm_row_ref, delta_row_ref = row_refs
    width = key_rows.shape[1]
    seq_len = query_ref.shape[0]
    cols = slice(head * width, (head + 1) * width)
    rows = slice(head * seq_len, (head + 1) * seq_len)
    weights_t, score_grad_t = score_blocks(
        key_rows, value_rows, query_t_ref[:, rows], grad_t_ref[:, rows],
        norm_row_ref[:, rows], delta_row_ref[:, rows], visible,
    )
    query_part = jnp.dot(key_t, score_grad_t, preferred_element_type=F32)
    key_part = jnp.dot(score_grad_t, query_ref[:, cols], preferred_element_type=F32)
    value_part = jnp.dot(weights_t, grad_rows_ref[:, cols], preferred_element_type=F32)
    return rows, cols, query_part, key_part, value_part


def suffix_kernel(*refs):
    row_refs, refs = refs[:6], refs[6:]
    query_acc_ref, key_ref, value_ref, query_grad_ref, key_grad_ref, value_grad_ref = refs
    seq_len, width = key_ref.shape
    key_at = lax.broadcasted_iota(jnp.int32, (seq_len, seq_len), 0)
    query_at = lax.broadcasted_iota(jnp.int32, (seq_len, seq_len), 1)
    causal = key_at <= query_at
    key_rows, value_rows = key_ref[...], value_ref[...]
    key_t = key_rows.T
    key_acc = jnp.zeros((seq_len, width), F32)
    value_acc = jnp.zeros((seq_len, width), F32)
    for head in range(query_grad_ref.shape[1] // width):
        rows, cols, query_part, key_part, value_part = attend_head(
            head, row_refs, key_rows, value_rows, key_t, causal
        )
        query_grad_ref[:, cols] = (query_part + query_acc_ref[:, rows]).T.astype(BF16)
        key_acc += key_part
        value_acc += value_part
    key_grad_ref[...] = key_acc.astype(BF16)
    value_grad_ref[...] = value_acc.astype(BF16)


def suffix_part(rows, query_acc, key_suffix, value_suffix):
    seq_len, width = key_suffix.shape
    suffix = jax.ShapeDtypeStruct(key_suffix.shape, BF16)
    return pl.pallas_call(
        suffix_kernel,
        in_specs=[VMEM] * (len(rows) + 3),
        out_specs=[VMEM] * 3,
        out_shape=[jax.ShapeDtypeStruct(rows[0].shape, BF16), suffix, suffix],
        compiler_params=PARAMS,
        cost_estimate=cost(query_acc.shape[1], seq_len, width),
        name="suffix_part",
    )(*rows, query_acc, key_suffix, value_suffix)


def prompt_kernel(info_ref, *refs, count, first):
    pair_refs, row_refs, refs = refs[:count], refs[count : count + 6], refs[count + 6 :]
    query_acc_ref = None if first else refs[0]
    query_out_ref, *pair_grad_refs = refs if first else refs[1:]
    chosen = info_ref[0]
    width = query_out_ref.shape[0]

    def rows_of(which):
        parts = [ref[:, chosen, which] for ref in pair_refs]
        return jnp.concatenate([part.reshape(-1, width) for part in parts], 0)

    key_rows, value_rows = rows_of(0), rows_of(1)
    key_t = key_rows.T
    key_acc = jnp.zeros(key_rows.shape, F32)
    value_acc = jnp.zeros(key_rows.shape, F32)
    for head in range(row_refs[0].shape[1] // width):
        rows, _, query_part, key_part, value_part = attend_head(
            head, row_refs, key_rows, value_rows, key_t
        )
        query_out_ref[:, rows] = query_part if first else query_part + query_acc_ref[:, rows]
        key_acc += key_part
        value_acc += value_part
    size = key_rows.shape[0] // count
    key_grad, value_grad = key_acc.astype(BF16), value_acc.astype(BF16)
    mark = jnp.full((MARK, width), chosen.astype(F32), F32).astype(BF16)
    for i, ref in enumerate(pair_grad_refs):
        ref[:size] = key_grad[i * size : (i + 1) * size]
        ref[size : 2 * size] = value_grad[i * size : (i + 1) * size]
        ref[2 * size :] = mark


def prompt_part(info, pairs, rows, query_acc=None):
    width, row_count = rows[2].shape
    stacks, _, _, owned, _ = pairs[0].shape
    size = stacks * owned
    out = jax.ShapeDtypeStruct((width, row_count), F32)
    pair_out = jax.ShapeDtypeStruct((2 * size + MARK, width), BF16)
    more = [] if query_acc is None else [query_acc]
    return pl.pallas_call(
        functools.partial(prompt_kernel, count=len(pairs), first=query_acc is None),
        in_specs=[SMEM] + [VMEM] * (len(pairs) + len(rows) + len(more)),
        out_specs=[VMEM] * (1 + len(pairs)),
        out_shape=[out] + [pair_out] * len(pairs),
        compiler_params=PARAMS,
        cost_estimate=cost(row_count, len(pairs) * size, width),
        name="prompt_part",
    )(info, *pairs, *rows, *more)


def group_kernel(*refs):
    share_refs, total_ref = refs[:-1], refs[-1]
    stacks, prompt_count, _, owned, width = total_ref.shape
    size = stacks * owned
    for which in range(2):
        rows = slice(which * size, (which + 1) * size)
        totals = [jnp.zeros((size, width), F32)] * prompt_count
        for ref in share_refs:
            share = ref[rows].astype(F32)
            mark = ref[2 * size :].astype(F32)[:1]
            for i in range(prompt_count):
                totals[i] += jnp.where(mark == float(i), share, 0.0)
        for i in range(prompt_count):
            total_ref[:, i, which] = totals[i].astype(BF16).reshape(stacks, owned, width)


def group_sum(shares, shape):
    return pl.pallas_call(
        group_kernel,
        in_specs=[VMEM] * len(shares),
        out_specs=VMEM,
        out_shape=jax.ShapeDtypeStruct(shape, BF16),
        compiler_params=PARAMS,
        name="group_sum",
    )(*shares)


def exchange(blocks, axes):
    return lax.all_to_all(blocks, axes, split_axis=0, concat_axis=0, tiled=True)


def trade(block, axis, target):
    return lax.ppermute(block, axis, [(i, target(i)) for i in range(lax.axis_size(axis))])


def per_device(
    query, key_suffix, value_suffix, key_prompt, value_prompt, attn_out, grad_out, log_norm,
    prompt_id, lengths,
):
    columns = query.shape[2]
    width = key_suffix.shape[2]
    prompt_count, owned = key_prompt.shape[:2]
    heads, stacks, lines = lax.axis_size("head"), lax.axis_size("z"), lax.axis_size("y")
    place = lax.axis_index("head")
    info = jnp.stack([prompt_id[0], place, lengths[0]]).astype(jnp.int32)

    stacked = exchange(spread(key_prompt, value_prompt, stacks).reshape(stacks, -1, width), "z")
    grads = []
    for i in range(heads):
        at = (place ^ i) * columns
        piece = lax.dynamic_slice_in_dim(grad_out[0], at, columns, axis=1)
        grads.append(trade(piece, "head", lambda j, i=i: j ^ i) if i else piece)
    stacked, info = lax.optimization_barrier((stacked, info))
    stacked = stacked.reshape(stacks, prompt_count, 2, owned, width)

    moved = {
        steps: trade(stacked, "y", lambda j, steps=steps: (j + steps) % lines)
        for steps in (1, lines - 1)
    }
    stacked, grads = lax.optimization_barrier((stacked, grads))
    other = trade(stacked, "c", lambda j: j ^ 1)
    rows = [query[0], *prepare(info, query[0], attn_out[0], log_norm[0], grads)]
    beside, rows[-1], source = lax.optimization_barrier(
        ([moved[1], moved[lines - 1]], rows[-1], stacked)
    )
    far = trade(source, "y", lambda j: (j + 2) % lines)
    beside_other = [trade(block, "c", lambda j: j ^ 1) for block in beside]

    shares = []

    def send(parts, places):
        for part, (steps, across) in zip(parts, places, strict=True):
            if not steps and not across:
                shares.append(part)
                continue
            target = lambda j, s=steps, o=across: 2 * ((j // 2 - s) % lines) + (j % 2 ^ o)
            shares.append(trade(part, GROUP, target))

    query_acc, *parts = prompt_part(info, [stacked, *beside, other], rows)
    far, query_acc = lax.optimization_barrier((far, query_acc))
    far_other = trade(far, "c", lambda j: j ^ 1)
    send(parts, [(0, 0), (1, 0), (lines - 1, 0), (0, 1)])
    query_acc, *parts = prompt_part(info, [far, far_other, *beside_other], rows, query_acc)
    parts, shares = lax.optimization_barrier((parts, shares))
    send(parts, [(2, 0), (2, 1), (1, 1), (lines - 1, 1)])

    query_grad, key_grad, value_grad = suffix_part(rows, query_acc, key_suffix[0], value_suffix[0])
    key_grad, shares = lax.optimization_barrier((key_grad, shares))

    totals = group_sum(shares, (stacks, prompt_count, 2, owned, width))
    final = exchange(totals.reshape(-1, prompt_count * 2 * owned, width), "z")
    final = jnp.sum(final.astype(F32), 0).astype(BF16)
    final = final.reshape(prompt_count, 2, owned, width)
    return (query_grad[None], key_grad[None], value_grad[None], final[:, 0], final[:, 1])


def solution(mesh):
    roll, head = mesh.devices.shape
    fine = Mesh(mesh.devices.reshape(roll // 8, 4, 2, head), ("z", "y", "c", "head"))
    rolls = ("z", "y", "c")
    by_rollout = P(rolls, None, "head")
    by_key = P(None, rolls, "head")
    by_row = P(rolls, "head", None)
    in_specs = (
        by_rollout, by_rollout, by_rollout, by_key, by_key, by_rollout, by_row, by_row,
        P(rolls), P(rolls),
    )
    out_specs = (by_rollout, by_rollout, by_rollout, by_key, by_key)
    return jax.shard_map(
        per_device, mesh=fine, in_specs=in_specs, out_specs=out_specs, check_vma=False
    )
```

```python
import functools

import jax
import jax.numpy as jnp
from jax import lax
from jax.experimental import pallas as pl
from jax.experimental.pallas import tpu as pltpu
from jax.sharding import Mesh
from jax.sharding import PartitionSpec as P

BF16 = jnp.bfloat16
F32 = jnp.float32
GROUP = ("y", "c")
LOG2E = 1.4426950408889634
VMEM = pl.BlockSpec(memory_space=pltpu.VMEM)
SMEM = pl.BlockSpec(memory_space=pltpu.SMEM)
PARAMS = pltpu.CompilerParams(vmem_limit_bytes=28 * 1024 * 1024)
MARK = 16


def cost(row_count, key_count, width):
    pairs = row_count * key_count
    return pl.CostEstimate(
        flops=10 * pairs * width, bytes_accessed=16 * row_count * width, transcendentals=pairs
    )


def score_blocks(key_rows, value_rows, query_t, grad_t, norm_row, delta_row, visible=None):
    scale = key_rows.shape[1] ** (-0.5)
    scores_t = jnp.dot(key_rows, query_t, preferred_element_type=F32)
    weights_t = jnp.exp2(scores_t * (scale * LOG2E) - norm_row)
    if visible is not None:
        weights_t = jnp.where(visible, weights_t, jnp.zeros_like(weights_t))
    weight_grad_t = jnp.dot(value_rows, grad_t, preferred_element_type=F32)
    score_grad_t = (weights_t * (weight_grad_t - delta_row) * scale).astype(BF16)
    return weights_t.astype(BF16), score_grad_t


def spread_kernel(key_ref, value_ref, out_ref):
    for i in range(out_ref.shape[0]):
        out_ref[i, :, 0] = key_ref[...]
        out_ref[i, :, 1] = value_ref[...]


def spread(keys, values, count):
    prompt_count, owned, width = keys.shape
    return pl.pallas_call(
        spread_kernel,
        in_specs=[VMEM] * 2,
        out_specs=VMEM,
        out_shape=jax.ShapeDtypeStruct((count, prompt_count, 2, owned, width), BF16),
        name="spread",
    )(keys, values)


def prepare_kernel(info_ref, query_ref, out_ref, norm_ref, *refs):
    grad_refs, refs = refs[:-5], refs[-5:]
    grad_rows_ref, query_t_ref, grad_t_ref, norm_row_ref, delta_row_ref = refs
    group_size, seq_len = norm_ref.shape
    width = query_ref.shape[1] // group_size
    part = grad_refs[0].shape[0]
    at = lax.broadcasted_iota(jnp.int32, grad_refs[0].shape, 0)
    for i, piece in enumerate(grad_refs):
        start = pl.multiple_of((info_ref[1] ^ i) * part, part)
        rows = piece[...]
        rows = jnp.where(at + start < info_ref[2], rows, jnp.zeros_like(rows))
        grad_rows_ref[pl.ds(start, part), :] = rows
    for head in range(group_size):
        cols = slice(head * width, (head + 1) * width)
        rows = slice(head * seq_len, (head + 1) * seq_len)
        grad_t = grad_rows_ref[:, cols].T
        out_t = out_ref[:, cols].T
        query_t_ref[:, rows] = query_ref[:, cols].T
        grad_t_ref[:, rows] = grad_t
        norm_row_ref[:, rows] = norm_ref[head : head + 1, :] * LOG2E
        delta_row_ref[:, rows] = jnp.sum(
            grad_t.astype(F32) * out_t.astype(F32), axis=0, keepdims=True
        )


def prepare(info, query, attn_out, log_norm, grads):
    group_size, seq_len = log_norm.shape
    width = query.shape[1] // group_size
    row_count = group_size * seq_len
    shape = jax.ShapeDtypeStruct
    return pl.pallas_call(
        prepare_kernel,
        in_specs=[SMEM] + [VMEM] * (3 + len(grads)),
        out_specs=[VMEM] * 5,
        out_shape=[
            shape(query.shape, BF16),
            shape((width, row_count), BF16),
            shape((width, row_count), BF16),
            shape((1, row_count), F32),
            shape((1, row_count), F32),
        ],
        compiler_params=PARAMS,
        cost_estimate=pl.CostEstimate(
            flops=2 * row_count * width, bytes_accessed=12 * row_count * width, transcendentals=0
        ),
        name="prepare",
    )(info, query, attn_out, log_norm, *grads)


def attend_heads(row_refs, key_rows, value_rows, emit, visible=None):
    query_ref, grad_rows_ref, query_t_ref, grad_t_ref, norm_row_ref, delta_row_ref = row_refs
    width = key_rows.shape[1]
    seq_len = query_ref.shape[0]
    head_count = query_ref.shape[1] // width
    key_t = key_rows.T
    key_acc = jnp.zeros(key_rows.shape, F32)
    value_acc = jnp.zeros(key_rows.shape, F32)

    def scores_of(head):
        rows = slice(head * seq_len, (head + 1) * seq_len)
        return score_blocks(
            key_rows, value_rows, query_t_ref[:, rows], grad_t_ref[:, rows],
            norm_row_ref[:, rows], delta_row_ref[:, rows], visible,
        )

    ahead = scores_of(0)
    for head in range(head_count):
        weights_t, score_grad_t = ahead
        if head + 1 < head_count:
            ahead = scores_of(head + 1)
        cols = slice(head * width, (head + 1) * width)
        rows = slice(head * seq_len, (head + 1) * seq_len)
        emit(rows, cols, jnp.dot(key_t, score_grad_t, preferred_element_type=F32))
        key_acc += jnp.dot(score_grad_t, query_ref[:, cols], preferred_element_type=F32)
        value_acc += jnp.dot(weights_t, grad_rows_ref[:, cols], preferred_element_type=F32)
    return key_acc.astype(BF16), value_acc.astype(BF16)


def suffix_kernel(*refs):
    row_refs, refs = refs[:6], refs[6:]
    query_acc_ref, key_ref, value_ref, query_grad_ref, key_grad_ref, value_grad_ref = refs
    seq_len, width = key_ref.shape
    key_at = lax.broadcasted_iota(jnp.int32, (seq_len, seq_len), 0)
    query_at = lax.broadcasted_iota(jnp.int32, (seq_len, seq_len), 1)
    causal = key_at <= query_at

    def emit(rows, cols, query_part):
        query_grad_ref[:, cols] = (query_part + query_acc_ref[:, rows]).T.astype(BF16)

    key_grad_ref[...], value_grad_ref[...] = attend_heads(
        row_refs, key_ref[...], value_ref[...], emit, causal
    )


def suffix_part(rows, query_acc, key_suffix, value_suffix):
    seq_len, width = key_suffix.shape
    suffix = jax.ShapeDtypeStruct(key_suffix.shape, BF16)
    return pl.pallas_call(
        suffix_kernel,
        in_specs=[VMEM] * (len(rows) + 3),
        out_specs=[VMEM] * 3,
        out_shape=[jax.ShapeDtypeStruct(rows[0].shape, BF16), suffix, suffix],
        compiler_params=PARAMS,
        cost_estimate=cost(query_acc.shape[1], seq_len, width),
        name="suffix_part",
    )(*rows, query_acc, key_suffix, value_suffix)


def prompt_kernel(info_ref, *refs, count, first):
    pair_refs, row_refs, refs = refs[:count], refs[count : count + 6], refs[count + 6 :]
    query_acc_ref = None if first else refs[0]
    query_out_ref, *pair_grad_refs = refs if first else refs[1:]
    chosen = info_ref[0]
    width = query_out_ref.shape[0]

    def rows_of(which):
        parts = [ref[:, chosen, which] for ref in pair_refs]
        return jnp.concatenate([part.reshape(-1, width) for part in parts], 0)

    def emit(rows, cols, query_part):
        query_out_ref[:, rows] = query_part if first else query_part + query_acc_ref[:, rows]

    key_grad, value_grad = attend_heads(row_refs, rows_of(0), rows_of(1), emit)
    size = key_grad.shape[0] // count
    mark = jnp.full((MARK, width), chosen.astype(F32), F32).astype(BF16)
    for i, ref in enumerate(pair_grad_refs):
        ref[:size] = key_grad[i * size : (i + 1) * size]
        ref[size : 2 * size] = value_grad[i * size : (i + 1) * size]
        ref[2 * size :] = mark


def prompt_part(info, pairs, rows, query_acc=None):
    width, row_count = rows[2].shape
    stacks, _, _, owned, _ = pairs[0].shape
    size = stacks * owned
    out = jax.ShapeDtypeStruct((width, row_count), F32)
    pair_out = jax.ShapeDtypeStruct((2 * size + MARK, width), BF16)
    more = [] if query_acc is None else [query_acc]
    return pl.pallas_call(
        functools.partial(prompt_kernel, count=len(pairs), first=query_acc is None),
        in_specs=[SMEM] + [VMEM] * (len(pairs) + len(rows) + len(more)),
        out_specs=[VMEM] * (1 + len(pairs)),
        out_shape=[out] + [pair_out] * len(pairs),
        compiler_params=PARAMS,
        cost_estimate=cost(row_count, len(pairs) * size, width),
        name="prompt_part",
    )(info, *pairs, *rows, *more)


def group_kernel(*refs):
    share_refs, total_ref = refs[:-1], refs[-1]
    stacks, prompt_count, _, owned, width = total_ref.shape
    size = stacks * owned
    for which in range(2):
        rows = slice(which * size, (which + 1) * size)
        totals = [jnp.zeros((size, width), F32)] * prompt_count
        for ref in share_refs:
            share = ref[rows].astype(F32)
            mark = ref[2 * size :].astype(F32)[:1]
            for i in range(prompt_count):
                totals[i] += jnp.where(mark == float(i), share, 0.0)
        for i in range(prompt_count):
            total_ref[:, i, which] = totals[i].astype(BF16).reshape(stacks, owned, width)


def group_sum(shares, shape):
    return pl.pallas_call(
        group_kernel,
        in_specs=[VMEM] * len(shares),
        out_specs=VMEM,
        out_shape=jax.ShapeDtypeStruct(shape, BF16),
        compiler_params=PARAMS,
        name="group_sum",
    )(*shares)


def exchange(blocks, axes):
    return lax.all_to_all(blocks, axes, split_axis=0, concat_axis=0, tiled=True)


def trade(block, axis, target):
    return lax.ppermute(block, axis, [(i, target(i)) for i in range(lax.axis_size(axis))])


def per_device(
    query, key_suffix, value_suffix, key_prompt, value_prompt, attn_out, grad_out, log_norm,
    prompt_id, lengths,
):
    columns = query.shape[2]
    width = key_suffix.shape[2]
    prompt_count, owned = key_prompt.shape[:2]
    heads, stacks, lines = lax.axis_size("head"), lax.axis_size("z"), lax.axis_size("y")
    place = lax.axis_index("head")
    info = jnp.stack([prompt_id[0], place, lengths[0]]).astype(jnp.int32)

    stacked = exchange(spread(key_prompt, value_prompt, stacks).reshape(stacks, -1, width), "z")
    grads = []
    for i in range(heads):
        at = (place ^ i) * columns
        piece = lax.dynamic_slice_in_dim(grad_out[0], at, columns, axis=1)
        grads.append(trade(piece, "head", lambda j, i=i: j ^ i) if i else piece)
    stacked, info = lax.optimization_barrier((stacked, info))
    stacked = stacked.reshape(stacks, prompt_count, 2, owned, width)

    moved = {
        steps: trade(stacked, "y", lambda j, steps=steps: (j + steps) % lines)
        for steps in (1, lines - 1)
    }
    stacked, grads = lax.optimization_barrier((stacked, grads))
    other = trade(stacked, "c", lambda j: j ^ 1)
    rows = [query[0], *prepare(info, query[0], attn_out[0], log_norm[0], grads)]
    beside, rows[-1], source = lax.optimization_barrier(
        ([moved[1], moved[lines - 1]], rows[-1], stacked)
    )
    far = trade(source, "y", lambda j: (j + 2) % lines)
    beside_other = [trade(block, "c", lambda j: j ^ 1) for block in beside]

    shares = []

    def send(parts, places):
        for part, (steps, across) in zip(parts, places, strict=True):
            if not steps and not across:
                shares.append(part)
                continue
            target = lambda j, s=steps, o=across: 2 * ((j // 2 - s) % lines) + (j % 2 ^ o)
            shares.append(trade(part, GROUP, target))

    query_acc, *parts = prompt_part(info, [stacked, *beside, other], rows)
    far, query_acc = lax.optimization_barrier((far, query_acc))
    far_other = trade(far, "c", lambda j: j ^ 1)
    send(parts, [(0, 0), (1, 0), (lines - 1, 0), (0, 1)])
    query_acc, *parts = prompt_part(info, [far, far_other], rows, query_acc)
    query_acc, beside_other, shares = lax.optimization_barrier((query_acc, beside_other, shares))
    send(parts, [(2, 0), (2, 1)])
    query_acc, *parts = prompt_part(info, beside_other, rows, query_acc)
    parts, shares = lax.optimization_barrier((parts, shares))
    send(parts, [(1, 1), (lines - 1, 1)])

    query_grad, key_grad, value_grad = suffix_part(rows, query_acc, key_suffix[0], value_suffix[0])
    key_grad, shares = lax.optimization_barrier((key_grad, shares))

    totals = group_sum(shares, (stacks, prompt_count, 2, owned, width))
    final = exchange(totals.reshape(-1, prompt_count * 2 * owned, width), "z")
    final = jnp.sum(final.astype(F32), 0).astype(BF16)
    final = final.reshape(prompt_count, 2, owned, width)
    return (query_grad[None], key_grad[None], value_grad[None], final[:, 0], final[:, 1])


def solution(mesh):
    roll, head = mesh.devices.shape
    fine = Mesh(mesh.devices.reshape(roll // 8, 4, 2, head), ("z", "y", "c", "head"))
    rolls = ("z", "y", "c")
    by_rollout = P(rolls, None, "head")
    by_key = P(None, rolls, "head")
    by_row = P(rolls, "head", None)
    in_specs = (
        by_rollout, by_rollout, by_rollout, by_key, by_key, by_rollout, by_row, by_row,
        P(rolls), P(rolls),
    )
    out_specs = (by_rollout, by_rollout, by_rollout, by_key, by_key)
    return jax.shard_map(
        per_device, mesh=fine, in_specs=in_specs, out_specs=out_specs, check_vma=False
    )
```

```python
import functools

import jax
import jax.numpy as jnp
from jax import lax
from jax.experimental import pallas as pl
from jax.experimental.pallas import tpu as pltpu
from jax.sharding import Mesh
from jax.sharding import PartitionSpec as P

BF16 = jnp.bfloat16
F32 = jnp.float32
GROUP = ("y", "c")
LOG2E = 1.4426950408889634
VMEM = pl.BlockSpec(memory_space=pltpu.VMEM)
SMEM = pl.BlockSpec(memory_space=pltpu.SMEM)
PARAMS = pltpu.CompilerParams(vmem_limit_bytes=28 * 1024 * 1024)
MARK = 16


def cost(row_count, key_count, width):
    pairs = row_count * key_count
    return pl.CostEstimate(
        flops=10 * pairs * width, bytes_accessed=16 * row_count * width, transcendentals=pairs
    )


def score_blocks(key_rows, value_rows, query_t, grad_t, norm_row, delta_row, visible=None):
    scale = key_rows.shape[1] ** (-0.5)
    scores_t = jnp.dot(key_rows, query_t, preferred_element_type=F32)
    weights_t = jnp.exp2(scores_t * (scale * LOG2E) - norm_row)
    if visible is not None:
        weights_t = jnp.where(visible, weights_t, jnp.zeros_like(weights_t))
    weight_grad_t = jnp.dot(value_rows, grad_t, preferred_element_type=F32)
    score_grad_t = (weights_t * (weight_grad_t - delta_row) * scale).astype(BF16)
    return weights_t.astype(BF16), score_grad_t


def spread_kernel(key_ref, value_ref, out_ref):
    for i in range(out_ref.shape[0]):
        out_ref[i, :, 0] = key_ref[...]
        out_ref[i, :, 1] = value_ref[...]


def spread(keys, values, count):
    prompt_count, owned, width = keys.shape
    return pl.pallas_call(
        spread_kernel,
        in_specs=[VMEM] * 2,
        out_specs=VMEM,
        out_shape=jax.ShapeDtypeStruct((count, prompt_count, 2, owned, width), BF16),
        name="spread",
    )(keys, values)


def prepare_kernel(info_ref, query_ref, out_ref, norm_ref, *refs):
    grad_refs, refs = refs[:-5], refs[-5:]
    grad_rows_ref, query_t_ref, grad_t_ref, norm_row_ref, delta_row_ref = refs
    group_size, seq_len = norm_ref.shape
    width = query_ref.shape[1] // group_size
    part = grad_refs[0].shape[0]
    at = lax.broadcasted_iota(jnp.int32, grad_refs[0].shape, 0)
    for i, piece in enumerate(grad_refs):
        start = pl.multiple_of((info_ref[1] ^ i) * part, part)
        rows = piece[...]
        rows = jnp.where(at + start < info_ref[2], rows, jnp.zeros_like(rows))
        grad_rows_ref[pl.ds(start, part), :] = rows
    for head in range(group_size):
        cols = slice(head * width, (head + 1) * width)
        rows = slice(head * seq_len, (head + 1) * seq_len)
        grad_t = grad_rows_ref[:, cols].T
        out_t = out_ref[:, cols].T
        query_t_ref[:, rows] = query_ref[:, cols].T
        grad_t_ref[:, rows] = grad_t
        norm_row_ref[:, rows] = norm_ref[head : head + 1, :] * LOG2E
        delta_row_ref[:, rows] = jnp.sum(
            grad_t.astype(F32) * out_t.astype(F32), axis=0, keepdims=True
        )


def prepare(info, query, attn_out, log_norm, grads):
    group_size, seq_len = log_norm.shape
    width = query.shape[1] // group_size
    row_count = group_size * seq_len
    shape = jax.ShapeDtypeStruct
    return pl.pallas_call(
        prepare_kernel,
        in_specs=[SMEM] + [VMEM] * (3 + len(grads)),
        out_specs=[VMEM] * 5,
        out_shape=[
            shape(query.shape, BF16),
            shape((width, row_count), BF16),
            shape((width, row_count), BF16),
            shape((1, row_count), F32),
            shape((1, row_count), F32),
        ],
        compiler_params=PARAMS,
        cost_estimate=pl.CostEstimate(
            flops=2 * row_count * width, bytes_accessed=12 * row_count * width, transcendentals=0
        ),
        name="prepare",
    )(info, query, attn_out, log_norm, *grads)


def attend_heads(row_refs, key_rows, value_rows, emit, visible=None):
    query_ref, grad_rows_ref, query_t_ref, grad_t_ref, norm_row_ref, delta_row_ref = row_refs
    width = key_rows.shape[1]
    seq_len = query_ref.shape[0]
    head_count = query_ref.shape[1] // width
    key_t = key_rows.T
    key_acc = jnp.zeros(key_rows.shape, F32)
    value_acc = jnp.zeros(key_rows.shape, F32)

    def scores_of(head):
        rows = slice(head * seq_len, (head + 1) * seq_len)
        return score_blocks(
            key_rows, value_rows, query_t_ref[:, rows], grad_t_ref[:, rows],
            norm_row_ref[:, rows], delta_row_ref[:, rows], visible,
        )

    ahead = scores_of(0)
    for head in range(head_count):
        weights_t, score_grad_t = ahead
        if head + 1 < head_count:
            ahead = scores_of(head + 1)
        cols = slice(head * width, (head + 1) * width)
        rows = slice(head * seq_len, (head + 1) * seq_len)
        emit(rows, cols, jnp.dot(key_t, score_grad_t, preferred_element_type=F32))
        key_acc += jnp.dot(score_grad_t, query_ref[:, cols], preferred_element_type=F32)
        value_acc += jnp.dot(weights_t, grad_rows_ref[:, cols], preferred_element_type=F32)
    return key_acc.astype(BF16), value_acc.astype(BF16)


def suffix_kernel(*refs):
    row_refs, refs = refs[:6], refs[6:]
    query_acc_ref, key_ref, value_ref, query_grad_ref, key_grad_ref, value_grad_ref = refs
    seq_len, width = key_ref.shape
    key_at = lax.broadcasted_iota(jnp.int32, (seq_len, seq_len), 0)
    query_at = lax.broadcasted_iota(jnp.int32, (seq_len, seq_len), 1)
    causal = key_at <= query_at

    def emit(rows, cols, query_part):
        query_grad_ref[:, cols] = (query_part + query_acc_ref[:, rows]).T.astype(BF16)

    key_grad_ref[...], value_grad_ref[...] = attend_heads(
        row_refs, key_ref[...], value_ref[...], emit, causal
    )


def suffix_part(rows, query_acc, key_suffix, value_suffix):
    seq_len, width = key_suffix.shape
    suffix = jax.ShapeDtypeStruct(key_suffix.shape, BF16)
    return pl.pallas_call(
        suffix_kernel,
        in_specs=[VMEM] * (len(rows) + 3),
        out_specs=[VMEM] * 3,
        out_shape=[jax.ShapeDtypeStruct(rows[0].shape, BF16), suffix, suffix],
        compiler_params=PARAMS,
        cost_estimate=cost(query_acc.shape[1], seq_len, width),
        name="suffix_part",
    )(*rows, query_acc, key_suffix, value_suffix)


def prompt_kernel(info_ref, *refs, count, first):
    pair_refs, row_refs, refs = refs[:count], refs[count : count + 6], refs[count + 6 :]
    query_acc_ref = None if first else refs[0]
    query_out_ref, *pair_grad_refs = refs if first else refs[1:]
    chosen = info_ref[0]
    width = query_out_ref.shape[0]

    def rows_of(which):
        parts = [ref[:, chosen, which] for ref in pair_refs]
        return jnp.concatenate([part.reshape(-1, width) for part in parts], 0)

    def emit(rows, cols, query_part):
        query_out_ref[:, rows] = query_part if first else query_part + query_acc_ref[:, rows]

    key_grad, value_grad = attend_heads(row_refs, rows_of(0), rows_of(1), emit)
    size = key_grad.shape[0] // count
    mark = jnp.full((MARK, width), chosen.astype(F32), F32).astype(BF16)
    for i, ref in enumerate(pair_grad_refs):
        ref[:size] = key_grad[i * size : (i + 1) * size]
        ref[size : 2 * size] = value_grad[i * size : (i + 1) * size]
        ref[2 * size :] = mark


def prompt_part(info, pairs, rows, query_acc=None):
    width, row_count = rows[2].shape
    stacks, _, _, owned, _ = pairs[0].shape
    size = stacks * owned
    out = jax.ShapeDtypeStruct((width, row_count), F32)
    pair_out = jax.ShapeDtypeStruct((2 * size + MARK, width), BF16)
    more = [] if query_acc is None else [query_acc]
    return pl.pallas_call(
        functools.partial(prompt_kernel, count=len(pairs), first=query_acc is None),
        in_specs=[SMEM] + [VMEM] * (len(pairs) + len(rows) + len(more)),
        out_specs=[VMEM] * (1 + len(pairs)),
        out_shape=[out] + [pair_out] * len(pairs),
        compiler_params=PARAMS,
        cost_estimate=cost(row_count, len(pairs) * size, width),
        name="prompt_part",
    )(info, *pairs, *rows, *more)


def group_kernel(*refs):
    share_refs, total_ref = refs[:-1], refs[-1]
    stacks, prompt_count, _, owned, width = total_ref.shape
    size = stacks * owned
    for which in range(2):
        rows = slice(which * size, (which + 1) * size)
        totals = [jnp.zeros((size, width), F32)] * prompt_count
        for ref in share_refs:
            share = ref[rows].astype(F32)
            mark = ref[2 * size :].astype(F32)[:1]
            for i in range(prompt_count):
                totals[i] += jnp.where(mark == float(i), share, 0.0)
        for i in range(prompt_count):
            total_ref[:, i, which] = totals[i].astype(BF16).reshape(stacks, owned, width)


def group_sum(shares, shape):
    return pl.pallas_call(
        group_kernel,
        in_specs=[VMEM] * len(shares),
        out_specs=VMEM,
        out_shape=jax.ShapeDtypeStruct(shape, BF16),
        compiler_params=PARAMS,
        name="group_sum",
    )(*shares)


def exchange(blocks, axes):
    return lax.all_to_all(blocks, axes, split_axis=0, concat_axis=0, tiled=True)


def trade(block, axis, target):
    return lax.ppermute(block, axis, [(i, target(i)) for i in range(lax.axis_size(axis))])


def per_device(
    query, key_suffix, value_suffix, key_prompt, value_prompt, attn_out, grad_out, log_norm,
    prompt_id, lengths,
):
    columns = query.shape[2]
    width = key_suffix.shape[2]
    prompt_count, owned = key_prompt.shape[:2]
    heads, stacks, lines = lax.axis_size("head"), lax.axis_size("z"), lax.axis_size("y")
    place = lax.axis_index("head")
    info = jnp.stack([prompt_id[0], place, lengths[0]]).astype(jnp.int32)

    stacked = exchange(spread(key_prompt, value_prompt, stacks).reshape(stacks, -1, width), "z")
    grads = []
    for i in range(heads):
        at = (place ^ i) * columns
        piece = lax.dynamic_slice_in_dim(grad_out[0], at, columns, axis=1)
        grads.append(trade(piece, "head", lambda j, i=i: j ^ i) if i else piece)
    stacked, info = lax.optimization_barrier((stacked, info))
    stacked = stacked.reshape(stacks, prompt_count, 2, owned, width)

    moved = {
        steps: trade(stacked, "y", lambda j, steps=steps: (j + steps) % lines)
        for steps in (1, lines - 1)
    }
    stacked, grads = lax.optimization_barrier((stacked, grads))
    other = trade(stacked, "c", lambda j: j ^ 1)
    rows = [query[0], *prepare(info, query[0], attn_out[0], log_norm[0], grads)]
    beside, rows[-1], source = lax.optimization_barrier(
        ([moved[1], moved[lines - 1]], rows[-1], stacked)
    )
    far = trade(source, "y", lambda j: (j + 2) % lines)
    beside_other = [trade(block, "c", lambda j: j ^ 1) for block in beside]

    shares = []

    def send(parts, places):
        parts, shares[:] = lax.optimization_barrier((parts, shares))
        for part, (steps, across) in zip(parts, places, strict=True):
            if not steps and not across:
                shares.append(part)
                continue
            target = lambda j, s=steps, o=across: 2 * ((j // 2 - s) % lines) + (j % 2 ^ o)
            shares.append(trade(part, GROUP, target))

    query_acc, *parts = prompt_part(info, [stacked, *beside, other], rows)
    far, query_acc = lax.optimization_barrier((far, query_acc))
    far_other = trade(far, "c", lambda j: j ^ 1)
    send(parts, [(0, 0), (1, 0), (lines - 1, 0), (0, 1)])
    query_acc, *parts = prompt_part(info, beside_other, rows, query_acc)
    query_acc, far_other = lax.optimization_barrier((query_acc, far_other))
    send(parts, [(1, 1), (lines - 1, 1)])
    query_acc, *parts = prompt_part(info, [far, far_other], rows, query_acc)
    send(parts, [(2, 0), (2, 1)])

    query_grad, key_grad, value_grad = suffix_part(rows, query_acc, key_suffix[0], value_suffix[0])
    key_grad, shares = lax.optimization_barrier((key_grad, shares))

    totals = group_sum(shares, (stacks, prompt_count, 2, owned, width))
    final = exchange(totals.reshape(-1, prompt_count * 2 * owned, width), "z")
    final = jnp.sum(final.astype(F32), 0).astype(BF16)
    final = final.reshape(prompt_count, 2, owned, width)
    return (query_grad[None], key_grad[None], value_grad[None], final[:, 0], final[:, 1])


def solution(mesh):
    roll, head = mesh.devices.shape
    fine = Mesh(mesh.devices.reshape(roll // 8, 4, 2, head), ("z", "y", "c", "head"))
    rolls = ("z", "y", "c")
    by_rollout = P(rolls, None, "head")
    by_key = P(None, rolls, "head")
    by_row = P(rolls, "head", None)
    in_specs = (
        by_rollout, by_rollout, by_rollout, by_key, by_key, by_rollout, by_row, by_row,
        P(rolls), P(rolls),
    )
    out_specs = (by_rollout, by_rollout, by_rollout, by_key, by_key)
    return jax.shard_map(
        per_device, mesh=fine, in_specs=in_specs, out_specs=out_specs, check_vma=False
    )
```

```python
import functools

import jax
import jax.numpy as jnp
from jax import lax
from jax.experimental import pallas as pl
from jax.experimental.pallas import tpu as pltpu
from jax.sharding import Mesh
from jax.sharding import PartitionSpec as P

BF16 = jnp.bfloat16
F32 = jnp.float32
GROUP = ("y", "c")
LOG2E = 1.4426950408889634
VMEM = pl.BlockSpec(memory_space=pltpu.VMEM)
SMEM = pl.BlockSpec(memory_space=pltpu.SMEM)
PARAMS = pltpu.CompilerParams(vmem_limit_bytes=28 * 1024 * 1024)
MARK = 16


def cost(row_count, key_count, width):
    pairs = row_count * key_count
    return pl.CostEstimate(
        flops=10 * pairs * width, bytes_accessed=16 * row_count * width, transcendentals=pairs
    )


def score_blocks(key_rows, value_rows, query_t, grad_t, norm_row, delta_row, visible=None):
    scale = key_rows.shape[1] ** (-0.5)
    scores_t = jnp.dot(key_rows, query_t, preferred_element_type=F32)
    weights_t = jnp.exp2(scores_t * (scale * LOG2E) - norm_row)
    if visible is not None:
        weights_t = jnp.where(visible, weights_t, jnp.zeros_like(weights_t))
    weight_grad_t = jnp.dot(value_rows, grad_t, preferred_element_type=F32)
    score_grad_t = (weights_t * (weight_grad_t - delta_row) * scale).astype(BF16)
    return weights_t.astype(BF16), score_grad_t


def spread_kernel(key_ref, value_ref, out_ref):
    for i in range(out_ref.shape[0]):
        out_ref[i, :, 0] = key_ref[...]
        out_ref[i, :, 1] = value_ref[...]


def spread(keys, values, count):
    prompt_count, owned, width = keys.shape
    return pl.pallas_call(
        spread_kernel,
        in_specs=[VMEM] * 2,
        out_specs=VMEM,
        out_shape=jax.ShapeDtypeStruct((count, prompt_count, 2, owned, width), BF16),
        name="spread",
    )(keys, values)


def prepare_kernel(info_ref, query_ref, out_ref, norm_ref, *refs):
    grad_refs, refs = refs[:-5], refs[-5:]
    grad_rows_ref, query_t_ref, grad_t_ref, norm_row_ref, delta_row_ref = refs
    group_size, seq_len = norm_ref.shape
    width = query_ref.shape[1] // group_size
    part = grad_refs[0].shape[0]
    at = lax.broadcasted_iota(jnp.int32, grad_refs[0].shape, 0)
    for i, piece in enumerate(grad_refs):
        start = pl.multiple_of((info_ref[1] ^ i) * part, part)
        rows = piece[...]
        rows = jnp.where(at + start < info_ref[2], rows, jnp.zeros_like(rows))
        grad_rows_ref[pl.ds(start, part), :] = rows
    for head in range(group_size):
        cols = slice(head * width, (head + 1) * width)
        rows = slice(head * seq_len, (head + 1) * seq_len)
        grad_t = grad_rows_ref[:, cols].T
        out_t = out_ref[:, cols].T
        query_t_ref[:, rows] = query_ref[:, cols].T
        grad_t_ref[:, rows] = grad_t
        norm_row_ref[:, rows] = norm_ref[head : head + 1, :] * LOG2E
        delta_row_ref[:, rows] = jnp.sum(
            grad_t.astype(F32) * out_t.astype(F32), axis=0, keepdims=True
        )


def prepare(info, query, attn_out, log_norm, grads):
    group_size, seq_len = log_norm.shape
    width = query.shape[1] // group_size
    row_count = group_size * seq_len
    shape = jax.ShapeDtypeStruct
    return pl.pallas_call(
        prepare_kernel,
        in_specs=[SMEM] + [VMEM] * (3 + len(grads)),
        out_specs=[VMEM] * 5,
        out_shape=[
            shape(query.shape, BF16),
            shape((width, row_count), BF16),
            shape((width, row_count), BF16),
            shape((1, row_count), F32),
            shape((1, row_count), F32),
        ],
        compiler_params=PARAMS,
        cost_estimate=pl.CostEstimate(
            flops=2 * row_count * width, bytes_accessed=12 * row_count * width, transcendentals=0
        ),
        name="prepare",
    )(info, query, attn_out, log_norm, *grads)


def attend_heads(row_refs, key_rows, value_rows, emit, visible=None):
    query_ref, grad_rows_ref, query_t_ref, grad_t_ref, norm_row_ref, delta_row_ref = row_refs
    width = key_rows.shape[1]
    seq_len = query_ref.shape[0]
    head_count = query_ref.shape[1] // width
    key_acc = jnp.zeros(key_rows.shape, F32)
    value_acc = jnp.zeros(key_rows.shape, F32)

    def scores_of(head):
        rows = slice(head * seq_len, (head + 1) * seq_len)
        return score_blocks(
            key_rows, value_rows, query_t_ref[:, rows], grad_t_ref[:, rows],
            norm_row_ref[:, rows], delta_row_ref[:, rows], visible,
        )

    ahead = scores_of(0)
    for head in range(head_count):
        weights_t, score_grad_t = ahead
        if head + 1 < head_count:
            ahead = scores_of(head + 1)
        cols = slice(head * width, (head + 1) * width)
        rows = slice(head * seq_len, (head + 1) * seq_len)
        emit(rows, cols, score_grad_t)
        key_acc += jnp.dot(score_grad_t, query_ref[:, cols], preferred_element_type=F32)
        value_acc += jnp.dot(weights_t, grad_rows_ref[:, cols], preferred_element_type=F32)
    return key_acc.astype(BF16), value_acc.astype(BF16)


def rows_of(pair_refs, chosen, which):
    parts = [ref[:, chosen, which] for ref in pair_refs]
    return jnp.concatenate([part.reshape(-1, part.shape[-1]) for part in parts], 0)


def suffix_kernel(info_ref, *refs, counts):
    row_refs, refs = refs[:6], refs[6:]
    chosen = info_ref[0]
    earlier = []
    for count in counts:
        earlier.append((rows_of(refs[:count], chosen, 0).T, refs[count]))
        refs = refs[count + 1 :]
    key_ref, value_ref, query_grad_ref, key_grad_ref, value_grad_ref = refs
    seq_len = key_ref.shape[0]
    key_at = lax.broadcasted_iota(jnp.int32, (seq_len, seq_len), 0)
    query_at = lax.broadcasted_iota(jnp.int32, (seq_len, seq_len), 1)
    causal = key_at <= query_at
    key_t = key_ref[...].T

    def emit(rows, cols, score_grad_t):
        total = jnp.dot(key_t, score_grad_t, preferred_element_type=F32)
        for prompt_key_t, score_ref in earlier:
            total += jnp.dot(prompt_key_t, score_ref[:, rows], preferred_element_type=F32)
        query_grad_ref[:, cols] = total.T.astype(BF16)

    key_grad_ref[...], value_grad_ref[...] = attend_heads(
        row_refs, key_ref[...], value_ref[...], emit, causal
    )


def suffix_part(info, rows, earlier, key_suffix, value_suffix):
    seq_len, width = key_suffix.shape
    suffix = jax.ShapeDtypeStruct(key_suffix.shape, BF16)
    flat = [item for pairs, scores in earlier for item in (*pairs, scores)]
    return pl.pallas_call(
        functools.partial(suffix_kernel, counts=[len(pairs) for pairs, _ in earlier]),
        in_specs=[SMEM] + [VMEM] * (len(rows) + len(flat) + 2),
        out_specs=[VMEM] * 3,
        out_shape=[jax.ShapeDtypeStruct(rows[0].shape, BF16), suffix, suffix],
        compiler_params=PARAMS,
        cost_estimate=cost(rows[2].shape[1], seq_len, width),
        name="suffix_part",
    )(info, *rows, *flat, key_suffix, value_suffix)


def prompt_kernel(info_ref, *refs, count):
    pair_refs, row_refs = refs[:count], refs[count : count + 6]
    score_out_ref, *pair_grad_refs = refs[count + 6 :]
    chosen = info_ref[0]
    width = pair_grad_refs[0].shape[1]

    def emit(rows, cols, score_grad_t):
        score_out_ref[:, rows] = score_grad_t

    keys, values = rows_of(pair_refs, chosen, 0), rows_of(pair_refs, chosen, 1)
    key_grad, value_grad = attend_heads(row_refs, keys, values, emit)
    size = key_grad.shape[0] // count
    mark = jnp.full((MARK, width), chosen.astype(F32), F32).astype(BF16)
    for i, ref in enumerate(pair_grad_refs):
        ref[:size] = key_grad[i * size : (i + 1) * size]
        ref[size : 2 * size] = value_grad[i * size : (i + 1) * size]
        ref[2 * size :] = mark


def prompt_part(info, pairs, rows):
    width, row_count = rows[2].shape
    stacks, _, _, owned, _ = pairs[0].shape
    size = stacks * owned
    pair_out = jax.ShapeDtypeStruct((2 * size + MARK, width), BF16)
    return pl.pallas_call(
        functools.partial(prompt_kernel, count=len(pairs)),
        in_specs=[SMEM] + [VMEM] * (len(pairs) + len(rows)),
        out_specs=[VMEM] * (1 + len(pairs)),
        out_shape=[jax.ShapeDtypeStruct((len(pairs) * size, row_count), BF16)]
        + [pair_out] * len(pairs),
        compiler_params=PARAMS,
        cost_estimate=cost(row_count, len(pairs) * size, width),
        name="prompt_part",
    )(info, *pairs, *rows)


def group_kernel(*refs):
    share_refs, total_ref = refs[:-1], refs[-1]
    stacks, prompt_count, _, owned, width = total_ref.shape
    size = stacks * owned
    for which in range(2):
        rows = slice(which * size, (which + 1) * size)
        totals = [jnp.zeros((size, width), F32)] * prompt_count
        for ref in share_refs:
            share = ref[rows].astype(F32)
            mark = ref[2 * size :].astype(F32)[:1]
            for i in range(prompt_count):
                totals[i] += jnp.where(mark == float(i), share, 0.0)
        for i in range(prompt_count):
            total_ref[:, i, which] = totals[i].astype(BF16).reshape(stacks, owned, width)


def group_sum(shares, shape):
    return pl.pallas_call(
        group_kernel,
        in_specs=[VMEM] * len(shares),
        out_specs=VMEM,
        out_shape=jax.ShapeDtypeStruct(shape, BF16),
        compiler_params=PARAMS,
        name="group_sum",
    )(*shares)


def exchange(blocks, axis):
    groups = [list(range(lax.axis_size(axis)))[::-1]]
    return lax.all_to_all(
        blocks, axis, split_axis=0, concat_axis=0, axis_index_groups=groups, tiled=True
    )


def trade(block, axis, target):
    return lax.ppermute(block, axis, [(i, target(i)) for i in range(lax.axis_size(axis))])


def per_device(
    query, key_suffix, value_suffix, key_prompt, value_prompt, attn_out, grad_out, log_norm,
    prompt_id, lengths,
):
    columns = query.shape[2]
    width = key_suffix.shape[2]
    prompt_count, owned = key_prompt.shape[:2]
    heads, stacks, lines = lax.axis_size("head"), lax.axis_size("z"), lax.axis_size("y")
    place = lax.axis_index("head")
    info = jnp.stack([prompt_id[0], place, lengths[0]]).astype(jnp.int32)

    stacked = exchange(spread(key_prompt, value_prompt, stacks).reshape(stacks, -1, width), "z")
    grads = []
    for i in range(heads):
        at = (place ^ i) * columns
        piece = lax.dynamic_slice_in_dim(grad_out[0], at, columns, axis=1)
        grads.append(trade(piece, "head", lambda j, i=i: j ^ i) if i else piece)
    stacked, info = lax.optimization_barrier((stacked, info))
    stacked = stacked.reshape(stacks, prompt_count, 2, owned, width)

    moved = {
        steps: trade(stacked, "y", lambda j, steps=steps: (j + steps) % lines)
        for steps in (1, lines - 1)
    }
    stacked, grads = lax.optimization_barrier((stacked, grads))
    other = trade(stacked, "c", lambda j: j ^ 1)
    rows = [query[0], *prepare(info, query[0], attn_out[0], log_norm[0], grads)]
    beside, rows[-1], source = lax.optimization_barrier(
        ([moved[1], moved[lines - 1]], rows[-1], stacked)
    )
    far = trade(source, "y", lambda j: (j + 2) % lines)
    beside_other = [trade(block, "c", lambda j: j ^ 1) for block in beside]

    shares = []

    def send(parts, places):
        for part, (steps, across) in zip(parts, places, strict=True):
            if not steps and not across:
                shares.append(part)
                continue
            target = lambda j, s=steps, o=across: 2 * ((j // 2 - s) % lines) + (j % 2 ^ o)
            shares.append(trade(part, GROUP, target))

    near = [stacked, *beside, other]
    near_scores, *parts = prompt_part(info, near, rows)
    far, parts = lax.optimization_barrier((far, parts))
    late = [far, trade(far, "c", lambda j: j ^ 1), *beside_other]
    send(parts, [(0, 0), (1, 0), (lines - 1, 0), (0, 1)])
    late_scores, *parts = prompt_part(info, late, rows)
    parts, shares = lax.optimization_barrier((parts, shares))
    send(parts, [(2, 0), (2, 1), (1, 1), (lines - 1, 1)])

    query_grad, key_grad, value_grad = suffix_part(
        info, rows, [(near, near_scores), (late, late_scores)], key_suffix[0], value_suffix[0]
    )
    key_grad, shares = lax.optimization_barrier((key_grad, shares))

    totals = group_sum(shares, (stacks, prompt_count, 2, owned, width))
    final = exchange(totals.reshape(-1, prompt_count * 2 * owned, width), "z")
    final = jnp.sum(final.astype(F32), 0).astype(BF16)
    final = final.reshape(prompt_count, 2, owned, width)
    return (query_grad[None], key_grad[None], value_grad[None], final[:, 0], final[:, 1])


def solution(mesh):
    roll, head = mesh.devices.shape
    fine = Mesh(mesh.devices.reshape(roll // 8, 4, 2, head), ("z", "y", "c", "head"))
    rolls = ("z", "y", "c")
    by_rollout = P(rolls, None, "head")
    by_key = P(None, rolls, "head")
    by_row = P(rolls, "head", None)
    in_specs = (
        by_rollout, by_rollout, by_rollout, by_key, by_key, by_rollout, by_row, by_row,
        P(rolls), P(rolls),
    )
    out_specs = (by_rollout, by_rollout, by_rollout, by_key, by_key)
    return jax.shard_map(
        per_device, mesh=fine, in_specs=in_specs, out_specs=out_specs, check_vma=False
    )
```

```python
import functools

import jax
import jax.numpy as jnp
from jax import lax
from jax.experimental import pallas as pl
from jax.experimental.pallas import tpu as pltpu
from jax.sharding import Mesh
from jax.sharding import PartitionSpec as P

BF16 = jnp.bfloat16
F32 = jnp.float32
GROUP = ("y", "c")
LOG2E = 1.4426950408889634
VMEM = pl.BlockSpec(memory_space=pltpu.VMEM)
SMEM = pl.BlockSpec(memory_space=pltpu.SMEM)
PARAMS = pltpu.CompilerParams(vmem_limit_bytes=28 * 1024 * 1024)
MARK = 16


def cost(row_count, key_count, width):
    pairs = row_count * key_count
    return pl.CostEstimate(
        flops=10 * pairs * width, bytes_accessed=16 * row_count * width, transcendentals=pairs
    )


def score_blocks(key_rows, value_rows, query_t, grad_t, norm_row, delta_row, visible=None):
    scale = key_rows.shape[1] ** (-0.5)
    scores_t = jnp.dot(key_rows, query_t, preferred_element_type=F32)
    weights_t = jnp.exp2(scores_t * (scale * LOG2E) - norm_row)
    if visible is not None:
        weights_t = jnp.where(visible, weights_t, jnp.zeros_like(weights_t))
    weight_grad_t = jnp.dot(value_rows, grad_t, preferred_element_type=F32)
    score_grad_t = (weights_t * (weight_grad_t - delta_row) * scale).astype(BF16)
    return weights_t.astype(BF16), score_grad_t


def spread_kernel(key_ref, value_ref, out_ref):
    for i in range(out_ref.shape[0]):
        out_ref[i, :, 0] = key_ref[...]
        out_ref[i, :, 1] = value_ref[...]


def spread(keys, values, count):
    prompt_count, owned, width = keys.shape
    return pl.pallas_call(
        spread_kernel,
        in_specs=[VMEM] * 2,
        out_specs=VMEM,
        out_shape=jax.ShapeDtypeStruct((count, prompt_count, 2, owned, width), BF16),
        name="spread",
    )(keys, values)


def prepare_kernel(info_ref, query_ref, out_ref, norm_ref, *refs):
    grad_refs, refs = refs[:-5], refs[-5:]
    grad_rows_ref, query_t_ref, grad_t_ref, norm_row_ref, delta_row_ref = refs
    group_size, seq_len = norm_ref.shape
    width = query_ref.shape[1] // group_size
    part = grad_refs[0].shape[0]
    at = lax.broadcasted_iota(jnp.int32, grad_refs[0].shape, 0)
    for i, piece in enumerate(grad_refs):
        start = pl.multiple_of((info_ref[1] ^ i) * part, part)
        rows = piece[...]
        rows = jnp.where(at + start < info_ref[2], rows, jnp.zeros_like(rows))
        grad_rows_ref[pl.ds(start, part), :] = rows
    for head in range(group_size):
        cols = slice(head * width, (head + 1) * width)
        rows = slice(head * seq_len, (head + 1) * seq_len)
        grad_t = grad_rows_ref[:, cols].T
        out_t = out_ref[:, cols].T
        query_t_ref[:, rows] = query_ref[:, cols].T
        grad_t_ref[:, rows] = grad_t
        norm_row_ref[:, rows] = norm_ref[head : head + 1, :] * LOG2E
        delta_row_ref[:, rows] = jnp.sum(
            grad_t.astype(F32) * out_t.astype(F32), axis=0, keepdims=True
        )


def prepare(info, query, attn_out, log_norm, grads):
    group_size, seq_len = log_norm.shape
    width = query.shape[1] // group_size
    row_count = group_size * seq_len
    shape = jax.ShapeDtypeStruct
    return pl.pallas_call(
        prepare_kernel,
        in_specs=[SMEM] + [VMEM] * (3 + len(grads)),
        out_specs=[VMEM] * 5,
        out_shape=[
            shape(query.shape, BF16),
            shape((width, row_count), BF16),
            shape((width, row_count), BF16),
            shape((1, row_count), F32),
            shape((1, row_count), F32),
        ],
        compiler_params=PARAMS,
        cost_estimate=pl.CostEstimate(
            flops=2 * row_count * width, bytes_accessed=12 * row_count * width, transcendentals=0
        ),
        name="prepare",
    )(info, query, attn_out, log_norm, *grads)


def attend_heads(row_refs, key_rows, value_rows, emit, visible=None):
    query_ref, grad_rows_ref, query_t_ref, grad_t_ref, norm_row_ref, delta_row_ref = row_refs
    width = key_rows.shape[1]
    seq_len = query_ref.shape[0]
    head_count = query_ref.shape[1] // width
    key_acc = jnp.zeros(key_rows.shape, F32)
    value_acc = jnp.zeros(key_rows.shape, F32)

    def scores_of(head):
        rows = slice(head * seq_len, (head + 1) * seq_len)
        return score_blocks(
            key_rows, value_rows, query_t_ref[:, rows], grad_t_ref[:, rows],
            norm_row_ref[:, rows], delta_row_ref[:, rows], visible,
        )

    ahead = scores_of(0)
    for head in range(head_count):
        weights_t, score_grad_t = ahead
        if head + 1 < head_count:
            ahead = scores_of(head + 1)
        cols = slice(head * width, (head + 1) * width)
        rows = slice(head * seq_len, (head + 1) * seq_len)
        emit(rows, cols, score_grad_t)
        key_acc += jnp.dot(score_grad_t, query_ref[:, cols], preferred_element_type=F32)
        value_acc += jnp.dot(weights_t, grad_rows_ref[:, cols], preferred_element_type=F32)
    return key_acc.astype(BF16), value_acc.astype(BF16)


def rows_of(pair_refs, chosen, which):
    parts = [ref[:, chosen, which] for ref in pair_refs]
    return jnp.concatenate([part.reshape(-1, part.shape[-1]) for part in parts], 0)


def suffix_kernel(info_ref, *refs, counts):
    row_refs, refs = refs[:6], refs[6:]
    chosen = info_ref[0]
    earlier = []
    for count in counts:
        earlier.append((rows_of(refs[:count], chosen, 0).T, refs[count]))
        refs = refs[count + 1 :]
    key_ref, value_ref, query_grad_ref, key_grad_ref, value_grad_ref = refs
    seq_len = key_ref.shape[0]
    key_at = lax.broadcasted_iota(jnp.int32, (seq_len, seq_len), 0)
    query_at = lax.broadcasted_iota(jnp.int32, (seq_len, seq_len), 1)
    causal = key_at <= query_at
    key_t = key_ref[...].T

    def emit(rows, cols, score_grad_t):
        total = jnp.dot(key_t, score_grad_t, preferred_element_type=F32)
        for prompt_key_t, score_ref in earlier:
            total += jnp.dot(prompt_key_t, score_ref[:, rows], preferred_element_type=F32)
        query_grad_ref[:, cols] = total.T.astype(BF16)

    key_grad_ref[...], value_grad_ref[...] = attend_heads(
        row_refs, key_ref[...], value_ref[...], emit, causal
    )


def suffix_part(info, rows, earlier, key_suffix, value_suffix):
    seq_len, width = key_suffix.shape
    suffix = jax.ShapeDtypeStruct(key_suffix.shape, BF16)
    flat = [item for pairs, scores in earlier for item in (*pairs, scores)]
    return pl.pallas_call(
        functools.partial(suffix_kernel, counts=[len(pairs) for pairs, _ in earlier]),
        in_specs=[SMEM] + [VMEM] * (len(rows) + len(flat) + 2),
        out_specs=[VMEM] * 3,
        out_shape=[jax.ShapeDtypeStruct(rows[0].shape, BF16), suffix, suffix],
        compiler_params=PARAMS,
        cost_estimate=cost(rows[2].shape[1], seq_len, width),
        name="suffix_part",
    )(info, *rows, *flat, key_suffix, value_suffix)


def prompt_kernel(info_ref, *refs, count):
    pair_refs, row_refs = refs[:count], refs[count : count + 6]
    score_out_ref, *pair_grad_refs = refs[count + 6 :]
    chosen = info_ref[0]
    width = pair_grad_refs[0].shape[1]

    def emit(rows, cols, score_grad_t):
        score_out_ref[:, rows] = score_grad_t

    keys, values = rows_of(pair_refs, chosen, 0), rows_of(pair_refs, chosen, 1)
    key_grad, value_grad = attend_heads(row_refs, keys, values, emit)
    size = key_grad.shape[0] // count
    mark = jnp.full((MARK, width), chosen.astype(F32), F32).astype(BF16)
    for i, ref in enumerate(pair_grad_refs):
        ref[:size] = key_grad[i * size : (i + 1) * size]
        ref[size : 2 * size] = value_grad[i * size : (i + 1) * size]
        ref[2 * size :] = mark


def prompt_part(info, pairs, rows):
    width, row_count = rows[2].shape
    stacks, _, _, owned, _ = pairs[0].shape
    size = stacks * owned
    pair_out = jax.ShapeDtypeStruct((2 * size + MARK, width), BF16)
    return pl.pallas_call(
        functools.partial(prompt_kernel, count=len(pairs)),
        in_specs=[SMEM] + [VMEM] * (len(pairs) + len(rows)),
        out_specs=[VMEM] * (1 + len(pairs)),
        out_shape=[jax.ShapeDtypeStruct((len(pairs) * size, row_count), BF16)]
        + [pair_out] * len(pairs),
        compiler_params=PARAMS,
        cost_estimate=cost(row_count, len(pairs) * size, width),
        name="prompt_part",
    )(info, *pairs, *rows)


def group_kernel(*refs):
    share_refs, total_ref = refs[:-1], refs[-1]
    stacks, prompt_count, _, owned, width = total_ref.shape
    size = stacks * owned
    for which in range(2):
        rows = slice(which * size, (which + 1) * size)
        totals = [jnp.zeros((size, width), F32)] * prompt_count
        for ref in share_refs:
            share = ref[rows].astype(F32)
            mark = ref[2 * size :].astype(F32)[:1]
            for i in range(prompt_count):
                totals[i] += jnp.where(mark == float(i), share, 0.0)
        for i in range(prompt_count):
            total_ref[:, i, which] = totals[i].astype(BF16).reshape(stacks, owned, width)


def group_sum(shares, shape):
    return pl.pallas_call(
        group_kernel,
        in_specs=[VMEM] * len(shares),
        out_specs=VMEM,
        out_shape=jax.ShapeDtypeStruct(shape, BF16),
        compiler_params=PARAMS,
        name="group_sum",
    )(*shares)


def exchange(blocks, axis):
    order = list(range(lax.axis_size(axis)))[::-1]
    order.insert(len(order) - 2, order.pop(2))
    return lax.all_to_all(
        blocks, axis, split_axis=0, concat_axis=0, axis_index_groups=[order], tiled=True
    )


def trade(block, axis, target):
    return lax.ppermute(block, axis, [(i, target(i)) for i in range(lax.axis_size(axis))])


def per_device(
    query, key_suffix, value_suffix, key_prompt, value_prompt, attn_out, grad_out, log_norm,
    prompt_id, lengths,
):
    columns = query.shape[2]
    width = key_suffix.shape[2]
    prompt_count, owned = key_prompt.shape[:2]
    heads, stacks, lines = lax.axis_size("head"), lax.axis_size("z"), lax.axis_size("y")
    place = lax.axis_index("head")
    info = jnp.stack([prompt_id[0], place, lengths[0]]).astype(jnp.int32)

    stacked = exchange(spread(key_prompt, value_prompt, stacks).reshape(stacks, -1, width), "z")
    grads = []
    for i in range(heads):
        at = (place ^ i) * columns
        piece = lax.dynamic_slice_in_dim(grad_out[0], at, columns, axis=1)
        grads.append(trade(piece, "head", lambda j, i=i: j ^ i) if i else piece)
    stacked, info = lax.optimization_barrier((stacked, info))
    stacked = stacked.reshape(stacks, prompt_count, 2, owned, width)

    moved = {
        steps: trade(stacked, "y", lambda j, steps=steps: (j + steps) % lines)
        for steps in (1, lines - 1)
    }
    stacked, grads = lax.optimization_barrier((stacked, grads))
    other = trade(stacked, "c", lambda j: j ^ 1)
    rows = [query[0], *prepare(info, query[0], attn_out[0], log_norm[0], grads)]
    beside, rows[-1], source = lax.optimization_barrier(
        ([moved[1], moved[lines - 1]], rows[-1], stacked)
    )
    far = trade(source, "y", lambda j: (j + 2) % lines)
    beside_other = [trade(block, "c", lambda j: j ^ 1) for block in beside]

    shares = []

    def send(parts, places):
        for part, (steps, across) in zip(parts, places, strict=True):
            if not steps and not across:
                shares.append(part)
                continue
            target = lambda j, s=steps, o=across: 2 * ((j // 2 - s) % lines) + (j % 2 ^ o)
            shares.append(trade(part, GROUP, target))

    near = [stacked, *beside, other]
    near_scores, *parts = prompt_part(info, near, rows)
    far, parts = lax.optimization_barrier((far, parts))
    late = [far, trade(far, "c", lambda j: j ^ 1), *beside_other]
    send(parts, [(0, 0), (1, 0), (lines - 1, 0), (0, 1)])
    late_scores, *parts = prompt_part(info, late, rows)
    parts, shares = lax.optimization_barrier((parts, shares))
    send(parts, [(2, 0), (2, 1), (1, 1), (lines - 1, 1)])

    query_grad, key_grad, value_grad = suffix_part(
        info, rows, [(near, near_scores), (late, late_scores)], key_suffix[0], value_suffix[0]
    )
    key_grad, shares = lax.optimization_barrier((key_grad, shares))

    totals = group_sum(shares, (stacks, prompt_count, 2, owned, width))
    final = exchange(totals.reshape(-1, prompt_count * 2 * owned, width), "z")
    final = jnp.sum(final.astype(F32), 0).astype(BF16)
    final = final.reshape(prompt_count, 2, owned, width)
    return (query_grad[None], key_grad[None], value_grad[None], final[:, 0], final[:, 1])


def solution(mesh):
    roll, head = mesh.devices.shape
    fine = Mesh(mesh.devices.reshape(roll // 8, 4, 2, head), ("z", "y", "c", "head"))
    rolls = ("z", "y", "c")
    by_rollout = P(rolls, None, "head")
    by_key = P(None, rolls, "head")
    by_row = P(rolls, "head", None)
    in_specs = (
        by_rollout, by_rollout, by_rollout, by_key, by_key, by_rollout, by_row, by_row,
        P(rolls), P(rolls),
    )
    out_specs = (by_rollout, by_rollout, by_rollout, by_key, by_key)
    return jax.shard_map(
        per_device, mesh=fine, in_specs=in_specs, out_specs=out_specs, check_vma=False
    )
```

```python
import functools

import jax
import jax.numpy as jnp
from jax import lax
from jax.experimental import pallas as pl
from jax.experimental.pallas import tpu as pltpu
from jax.sharding import Mesh
from jax.sharding import PartitionSpec as P

BF16 = jnp.bfloat16
F32 = jnp.float32
GROUP = ("y", "c")
LOG2E = 1.4426950408889634
VMEM = pl.BlockSpec(memory_space=pltpu.VMEM)
SMEM = pl.BlockSpec(memory_space=pltpu.SMEM)
PARAMS = pltpu.CompilerParams(vmem_limit_bytes=28 * 1024 * 1024)
MARK = 16


def cost(row_count, key_count, width):
    pairs = row_count * key_count
    return pl.CostEstimate(
        flops=10 * pairs * width, bytes_accessed=16 * row_count * width, transcendentals=pairs
    )


def score_blocks(key_rows, value_rows, query_t, grad_t, norm_row, delta_row, visible=None):
    scale = key_rows.shape[1] ** (-0.5)
    scores_t = jnp.dot(key_rows, query_t, preferred_element_type=F32)
    weights_t = jnp.exp2(scores_t * (scale * LOG2E) - norm_row)
    if visible is not None:
        weights_t = jnp.where(visible, weights_t, jnp.zeros_like(weights_t))
    weight_grad_t = jnp.dot(value_rows, grad_t, preferred_element_type=F32)
    score_grad_t = (weights_t * (weight_grad_t - delta_row) * scale).astype(BF16)
    return weights_t.astype(BF16), score_grad_t


def spread_kernel(key_ref, value_ref, out_ref):
    for i in range(out_ref.shape[0]):
        out_ref[i, :, 0] = key_ref[...]
        out_ref[i, :, 1] = value_ref[...]


def spread(keys, values, count):
    prompt_count, owned, width = keys.shape
    return pl.pallas_call(
        spread_kernel,
        in_specs=[VMEM] * 2,
        out_specs=VMEM,
        out_shape=jax.ShapeDtypeStruct((count, prompt_count, 2, owned, width), BF16),
        name="spread",
    )(keys, values)


def prepare_kernel(info_ref, query_ref, out_ref, norm_ref, *refs):
    grad_refs, refs = refs[:-5], refs[-5:]
    grad_rows_ref, query_t_ref, grad_t_ref, norm_row_ref, delta_row_ref = refs
    group_size, seq_len = norm_ref.shape
    width = query_ref.shape[1] // group_size
    part = grad_refs[0].shape[0]
    at = lax.broadcasted_iota(jnp.int32, grad_refs[0].shape, 0)
    for i, piece in enumerate(grad_refs):
        start = pl.multiple_of((info_ref[1] ^ i) * part, part)
        rows = piece[...]
        rows = jnp.where(at + start < info_ref[2], rows, jnp.zeros_like(rows))
        grad_rows_ref[pl.ds(start, part), :] = rows
    for head in range(group_size):
        cols = slice(head * width, (head + 1) * width)
        rows = slice(head * seq_len, (head + 1) * seq_len)
        grad_t = grad_rows_ref[:, cols].T
        out_t = out_ref[:, cols].T
        query_t_ref[:, rows] = query_ref[:, cols].T
        grad_t_ref[:, rows] = grad_t
        norm_row_ref[:, rows] = norm_ref[head : head + 1, :] * LOG2E
        delta_row_ref[:, rows] = jnp.sum(
            grad_t.astype(F32) * out_t.astype(F32), axis=0, keepdims=True
        )


def prepare(info, query, attn_out, log_norm, grads):
    group_size, seq_len = log_norm.shape
    width = query.shape[1] // group_size
    row_count = group_size * seq_len
    shape = jax.ShapeDtypeStruct
    return pl.pallas_call(
        prepare_kernel,
        in_specs=[SMEM] + [VMEM] * (3 + len(grads)),
        out_specs=[VMEM] * 5,
        out_shape=[
            shape(query.shape, BF16),
            shape((width, row_count), BF16),
            shape((width, row_count), BF16),
            shape((1, row_count), F32),
            shape((1, row_count), F32),
        ],
        compiler_params=PARAMS,
        cost_estimate=pl.CostEstimate(
            flops=2 * row_count * width, bytes_accessed=12 * row_count * width, transcendentals=0
        ),
        name="prepare",
    )(info, query, attn_out, log_norm, *grads)


def attend_heads(row_refs, key_rows, value_rows, emit, visible=None):
    query_ref, grad_rows_ref, query_t_ref, grad_t_ref, norm_row_ref, delta_row_ref = row_refs
    width = key_rows.shape[1]
    seq_len = query_ref.shape[0]
    head_count = query_ref.shape[1] // width
    key_acc = jnp.zeros(key_rows.shape, F32)
    value_acc = jnp.zeros(key_rows.shape, F32)

    def scores_of(head):
        rows = slice(head * seq_len, (head + 1) * seq_len)
        return score_blocks(
            key_rows, value_rows, query_t_ref[:, rows], grad_t_ref[:, rows],
            norm_row_ref[:, rows], delta_row_ref[:, rows], visible,
        )

    ahead = scores_of(0)
    for head in range(head_count):
        weights_t, score_grad_t = ahead
        if head + 1 < head_count:
            ahead = scores_of(head + 1)
        cols = slice(head * width, (head + 1) * width)
        rows = slice(head * seq_len, (head + 1) * seq_len)
        emit(rows, cols, score_grad_t)
        key_acc += jnp.dot(score_grad_t, query_ref[:, cols], preferred_element_type=F32)
        value_acc += jnp.dot(weights_t, grad_rows_ref[:, cols], preferred_element_type=F32)
    return key_acc.astype(BF16), value_acc.astype(BF16)


def rows_of(pair_refs, chosen, which):
    parts = [ref[:, chosen, which] for ref in pair_refs]
    return jnp.concatenate([part.reshape(-1, part.shape[-1]) for part in parts], 0)


def suffix_kernel(info_ref, *refs, counts):
    row_refs, refs = refs[:6], refs[6:]
    chosen = info_ref[0]
    earlier = []
    for count in counts:
        earlier.append((rows_of(refs[:count], chosen, 0).T, refs[count]))
        refs = refs[count + 1 :]
    key_ref, value_ref, query_grad_ref, key_grad_ref, value_grad_ref = refs
    seq_len = key_ref.shape[0]
    key_at = lax.broadcasted_iota(jnp.int32, (seq_len, seq_len), 0)
    query_at = lax.broadcasted_iota(jnp.int32, (seq_len, seq_len), 1)
    causal = key_at <= query_at
    key_t = key_ref[...].T

    def emit(rows, cols, score_grad_t):
        total = jnp.dot(key_t, score_grad_t, preferred_element_type=F32)
        for prompt_key_t, score_ref in earlier:
            total += jnp.dot(prompt_key_t, score_ref[:, rows], preferred_element_type=F32)
        query_grad_ref[:, cols] = total.T.astype(BF16)

    key_grad_ref[...], value_grad_ref[...] = attend_heads(
        row_refs, key_ref[...], value_ref[...], emit, causal
    )


def suffix_part(info, rows, earlier, key_suffix, value_suffix):
    seq_len, width = key_suffix.shape
    suffix = jax.ShapeDtypeStruct(key_suffix.shape, BF16)
    flat = [item for pairs, scores in earlier for item in (*pairs, scores)]
    return pl.pallas_call(
        functools.partial(suffix_kernel, counts=[len(pairs) for pairs, _ in earlier]),
        in_specs=[SMEM] + [VMEM] * (len(rows) + len(flat) + 2),
        out_specs=[VMEM] * 3,
        out_shape=[jax.ShapeDtypeStruct(rows[0].shape, BF16), suffix, suffix],
        compiler_params=PARAMS,
        cost_estimate=cost(rows[2].shape[1], seq_len, width),
        name="suffix_part",
    )(info, *rows, *flat, key_suffix, value_suffix)


def prompt_kernel(info_ref, *refs, count):
    pair_refs, row_refs = refs[:count], refs[count : count + 6]
    score_out_ref, *pair_grad_refs = refs[count + 6 :]
    chosen = info_ref[0]
    width = pair_grad_refs[0].shape[1]

    def emit(rows, cols, score_grad_t):
        score_out_ref[:, rows] = score_grad_t

    keys, values = rows_of(pair_refs, chosen, 0), rows_of(pair_refs, chosen, 1)
    key_grad, value_grad = attend_heads(row_refs, keys, values, emit)
    size = key_grad.shape[0] // count
    mark = jnp.full((MARK, width), chosen.astype(F32), F32).astype(BF16)
    for i, ref in enumerate(pair_grad_refs):
        ref[:size] = key_grad[i * size : (i + 1) * size]
        ref[size : 2 * size] = value_grad[i * size : (i + 1) * size]
        ref[2 * size :] = mark


def prompt_part(info, pairs, rows):
    width, row_count = rows[2].shape
    stacks, _, _, owned, _ = pairs[0].shape
    size = stacks * owned
    pair_out = jax.ShapeDtypeStruct((2 * size + MARK, width), BF16)
    return pl.pallas_call(
        functools.partial(prompt_kernel, count=len(pairs)),
        in_specs=[SMEM] + [VMEM] * (len(pairs) + len(rows)),
        out_specs=[VMEM] * (1 + len(pairs)),
        out_shape=[jax.ShapeDtypeStruct((len(pairs) * size, row_count), BF16)]
        + [pair_out] * len(pairs),
        compiler_params=PARAMS,
        cost_estimate=cost(row_count, len(pairs) * size, width),
        name="prompt_part",
    )(info, *pairs, *rows)


def group_kernel(*refs):
    share_refs, total_ref = refs[:-1], refs[-1]
    stacks, prompt_count, _, owned, width = total_ref.shape
    size = stacks * owned
    for which in range(2):
        rows = slice(which * size, (which + 1) * size)
        totals = [jnp.zeros((size, width), F32)] * prompt_count
        for ref in share_refs:
            share = ref[rows].astype(F32)
            mark = ref[2 * size :].astype(F32)[:1]
            for i in range(prompt_count):
                totals[i] += jnp.where(mark == float(i), share, 0.0)
        for i in range(prompt_count):
            total_ref[:, i, which] = totals[i].astype(BF16).reshape(stacks, owned, width)


def group_sum(shares, shape):
    return pl.pallas_call(
        group_kernel,
        in_specs=[VMEM] * len(shares),
        out_specs=VMEM,
        out_shape=jax.ShapeDtypeStruct(shape, BF16),
        compiler_params=PARAMS,
        name="group_sum",
    )(*shares)


def exchange(blocks, axis):
    order = list(range(lax.axis_size(axis)))[::-1]
    order.insert(len(order) - 2, order.pop(len(order) - 3))
    return lax.all_to_all(
        blocks, axis, split_axis=0, concat_axis=0, axis_index_groups=[order], tiled=True
    )


def trade(block, axis, target):
    return lax.ppermute(block, axis, [(i, target(i)) for i in range(lax.axis_size(axis))])


def per_device(
    query, key_suffix, value_suffix, key_prompt, value_prompt, attn_out, grad_out, log_norm,
    prompt_id, lengths,
):
    columns = query.shape[2]
    width = key_suffix.shape[2]
    prompt_count, owned = key_prompt.shape[:2]
    heads, stacks, lines = lax.axis_size("head"), lax.axis_size("z"), lax.axis_size("y")
    place = lax.axis_index("head")
    info = jnp.stack([prompt_id[0], place, lengths[0]]).astype(jnp.int32)

    stacked = exchange(spread(key_prompt, value_prompt, stacks).reshape(stacks, -1, width), "z")
    grads = []
    for i in range(heads):
        at = (place ^ i) * columns
        piece = lax.dynamic_slice_in_dim(grad_out[0], at, columns, axis=1)
        grads.append(trade(piece, "head", lambda j, i=i: j ^ i) if i else piece)
    stacked, info = lax.optimization_barrier((stacked, info))
    stacked = stacked.reshape(stacks, prompt_count, 2, owned, width)

    moved = {
        steps: trade(stacked, "y", lambda j, steps=steps: (j + steps) % lines)
        for steps in (1, lines - 1)
    }
    stacked, grads = lax.optimization_barrier((stacked, grads))
    other = trade(stacked, "c", lambda j: j ^ 1)
    rows = [query[0], *prepare(info, query[0], attn_out[0], log_norm[0], grads)]
    beside, rows[-1], source = lax.optimization_barrier(
        ([moved[1], moved[lines - 1]], rows[-1], stacked)
    )
    far = trade(source, "y", lambda j: (j + 2) % lines)
    beside_other = [trade(block, "c", lambda j: j ^ 1) for block in beside]

    shares = []

    def send(parts, places):
        for part, (steps, across) in zip(parts, places, strict=True):
            if not steps and not across:
                shares.append(part)
                continue
            target = lambda j, s=steps, o=across: 2 * ((j // 2 - s) % lines) + (j % 2 ^ o)
            shares.append(trade(part, GROUP, target))

    near = [stacked, *beside, other]
    near_scores, *parts = prompt_part(info, near, rows)
    far, parts = lax.optimization_barrier((far, parts))
    late = [far, trade(far, "c", lambda j: j ^ 1), *beside_other]
    send(parts, [(0, 0), (1, 0), (lines - 1, 0), (0, 1)])
    late_scores, *parts = prompt_part(info, late, rows)
    parts, shares = lax.optimization_barrier((parts, shares))
    send(parts, [(2, 0), (2, 1), (1, 1), (lines - 1, 1)])

    query_grad, key_grad, value_grad = suffix_part(
        info, rows, [(near, near_scores), (late, late_scores)], key_suffix[0], value_suffix[0]
    )
    key_grad, shares = lax.optimization_barrier((key_grad, shares))

    totals = group_sum(shares, (stacks, prompt_count, 2, owned, width))
    final = exchange(totals.reshape(-1, prompt_count * 2 * owned, width), "z")
    final = jnp.sum(final.astype(F32), 0).astype(BF16)
    final = final.reshape(prompt_count, 2, owned, width)
    return (query_grad[None], key_grad[None], value_grad[None], final[:, 0], final[:, 1])


def solution(mesh):
    roll, head = mesh.devices.shape
    fine = Mesh(mesh.devices.reshape(roll // 8, 4, 2, head), ("z", "y", "c", "head"))
    rolls = ("z", "y", "c")
    by_rollout = P(rolls, None, "head")
    by_key = P(None, rolls, "head")
    by_row = P(rolls, "head", None)
    in_specs = (
        by_rollout, by_rollout, by_rollout, by_key, by_key, by_rollout, by_row, by_row,
        P(rolls), P(rolls),
    )
    out_specs = (by_rollout, by_rollout, by_rollout, by_key, by_key)
    return jax.shard_map(
        per_device, mesh=fine, in_specs=in_specs, out_specs=out_specs, check_vma=False
    )
```
